32 devices in a mesh: snap: 2 (over y), brick: 16 (over z, x, core).
Axes of the slice: x: 2, y: 2, z: 4, core: 2. Of those that a mesh axis runs over, the one named last changes fastest.
Arguments:
- positions: float32 [2, 3, 4096], P('snap', None, 'brick'), may hold values from 0 to 7, as said below
- species: int32 [2, 4096], P('snap', 'brick'), may hold values from 0 to 4
- atom_words: int32 [2, 4096], P('snap', 'brick'), may hold values from 0 to 32767, as said below
- left_vector: float32 [2, 3, 4096], P('snap', None, 'brick'), may hold values from -6 to 6
- right_vector: float32 [5, 81, 80], replicated, may hold values from -0.006 to 0.006
- direction: float32 [5, 81, 80], replicated, may hold values from -6 to 6
- solution: float32 [5, 81, 80], replicated, may hold values from -6 to 6
- scalars: float32 [3], replicated, may hold values from 0.0005 to 2, as said below
Outputs:
- left_next: float32 [2, 3, 4096], P('snap', None, 'brick')
- right_next: float32 [5, 81, 80], replicated
- direction_next: float32 [5, 81, 80], replicated
- solution_next: float32 [5, 81, 80], replicated
- scalars_next: float32 [3], replicated
The draws below stay inside these ranges and needn't reach their ends.
Inputs may be any that keep to these rules, and one draw needn't show every extreme that they name: `atom_words`: bit o-1 of atom g's word (o = 1..15) marks g+o as its neighbour; no bit points outside the snapshot. `positions`: rows 0 and 1 are transverse coordinates; row 2 is the offset along the column, below 0.2. `scalars`: alpha lies between 0.0005 and 0.002; rho_bar and phi_bar between 0.5 and 2.
All inputs are finite; a program needn't handle non-finite values.
Results may differ from the reference program's by a relative error of at most 0.0003.
Values sent between devices are 32-bit elements; how exact they have to be, the bound alone decides.
A program may use at most 64 MiB of HBM per device.

```python
import math
import jax
import jax.numpy as jnp
from jax import lax

SPECIES = 5
RADIAL = 16
WINDOW = 15
ITERS = 3
CHANNELS = 80
SNAPS = 2
NATOMS = 4096


def draw_positions(key, part):
    plane_key, shift_key = jax.random.split(jax.random.fold_in(key, 11))
    atom_index = jnp.arange(NATOMS, dtype=jnp.float32)
    column_width = 3.5 + 3.5 * atom_index / NATOMS
    plane_coords = jax.random.uniform(plane_key, (SNAPS, 2, NATOMS), jnp.float32)
    shifts = 0.2 * jax.random.uniform(shift_key, (SNAPS, 1, NATOMS), jnp.float32)
    return jnp.concatenate([plane_coords * column_width[None, None, :], shifts], axis=1)


def draw_atom_words(key, part):
    upward = jax.random.randint(jax.random.fold_in(key, 23), (SNAPS, NATOMS), 0, 2 ** WINDOW, dtype=jnp.int32)
    atom_index = jnp.arange(NATOMS, dtype=jnp.int32)
    middle = NATOMS // 2
    full_run = (atom_index >= middle - WINDOW) & (atom_index <= middle)
    upward = jnp.where(full_run[None, :], 2 ** WINDOW - 1, upward)
    packed = jnp.zeros((SNAPS, NATOMS), jnp.int32)
    for offset in range(1, WINDOW + 1):
        inside = (atom_index + offset < NATOMS).astype(jnp.int32)
        upper_bit = jnp.bitwise_and(jnp.right_shift(upward, offset - 1), 1) * inside[None, :]
        packed = packed + upper_bit * 2 ** (offset - 1)
    return packed


def draw_scalars(key, part):
    first = jax.random.uniform(jax.random.fold_in(key, 31), (1,), jnp.float32, 0.0005, 0.002)
    rest = jax.random.uniform(jax.random.fold_in(key, 37), (2,), jnp.float32, 0.5, 2.0)
    return jnp.concatenate([first, rest])


def with_ends(drawn, key, smallest, top_value):
    longest = drawn.shape.index(max(drawn.shape))
    spots = []
    for shift in (0, 1):
        where = [jax.random.randint(jax.random.fold_in(key, axis), (), 0, length) for axis, length in enumerate(drawn.shape)]
        where[longest] = (where[longest] + shift) % drawn.shape[longest]
        spots.append(tuple(where))
    return drawn.at[spots[0]].set(smallest).at[spots[1]].set(top_value)


def level_of(rng, shape, cuts, least, top_value):
    gain = 1.0
    for dim, blocks in cuts:
        steps = jax.random.uniform(jax.random.fold_in(jax.random.fold_in(rng, 6), dim), (blocks,), jnp.float32, least / len(cuts), top_value / len(cuts))
        gain = gain * jnp.repeat(jnp.exp(steps), shape[dim] // blocks).reshape((-1,) + (1,) * (len(shape) - 1 - dim))
    return gain


def centred(own_key, dims, deviation, limit, cuts=(), kind=jnp.bfloat16):
    loudness = level_of(own_key, dims, cuts, -0.22, 0.18) if cuts else 1.0
    values = jax.random.normal(own_key, dims, jnp.float32) * deviation * loudness
    return jnp.minimum(jnp.maximum(values, -limit), limit).astype(kind)


def setup_inputs(seed: int = 0) -> dict:
    seeds = jax.random.split(jax.random.key(seed), 9)
    positions = draw_positions(jax.random.fold_in(seeds[8], 71), 0)
    species = with_ends(jax.random.randint(seeds[1], (SNAPS, NATOMS), 0, SPECIES), jax.random.fold_in(seeds[1], 1), 0, SPECIES - 1).astype(jnp.int32)
    atom_words = draw_atom_words(jax.random.fold_in(seeds[8], 71), 0)
    left_vector = centred(seeds[3], (SNAPS, 3, NATOMS), 1.0, 6.0, ((0, 2), (2, 16)), jnp.float32)
    right_vector = centred(seeds[4], (SPECIES, CHANNELS + 1, CHANNELS), 0.001, 0.006, (), jnp.float32)
    direction = centred(seeds[5], (SPECIES, CHANNELS + 1, CHANNELS), 1.0, 6.0, (), jnp.float32)
    solution = centred(seeds[6], (SPECIES, CHANNELS + 1, CHANNELS), 1.0, 6.0, (), jnp.float32)
    scalars = draw_scalars(jax.random.fold_in(seeds[8], 71), 0)
    return dict(positions=positions, species=species, atom_words=atom_words, left_vector=left_vector, right_vector=right_vector, direction=direction, solution=solution, scalars=scalars)


cutoff_sq = 36.0
spacing = 0.25
force_unit = 0.015625
tiny = 1e-06
HIGHEST = lax.Precision.HIGHEST

def window_offsets():
    return [shift_by for shift_by in range(1, WINDOW + 1)] + [-shift_by for shift_by in range(1, WINDOW + 1)]

def radial_tables(scaled):
    envelope = jnp.maximum(1.0 - scaled, 0.0)
    argument = 2.0 * jnp.minimum(scaled, 1.0) - 1.0
    first_kind = [jnp.ones_like(argument), argument]
    second_kind = [jnp.ones_like(argument), 2.0 * argument]
    for degree in range(2, RADIAL):
        first_kind.append(2.0 * argument * first_kind[-1] - first_kind[-2])
        second_kind.append(2.0 * argument * second_kind[-1] - second_kind[-2])
    values = []
    slopes = []
    for degree in range(RADIAL):
        damping = 1.0 / (1.0 + degree)
        values.append(envelope * envelope * first_kind[degree] * damping)
        derivative = -2.0 * envelope * first_kind[degree]
        if degree > 0:
            derivative = derivative + 2.0 * degree * envelope * envelope * second_kind[degree - 1]
        slopes.append(derivative * damping)
    return (jnp.stack(values, axis=1), jnp.stack(slopes, axis=1))

def shifted_stack(padded, atom_count):
    return jnp.stack([padded[:, WINDOW + offset:WINDOW + offset + atom_count] for offset in window_offsets()])

def pair_tables(padded, atom_count):
    offsets = window_offsets()
    here = padded[:, WINDOW:WINDOW + atom_count]
    there = shifted_stack(padded, atom_count)
    lift = jnp.array([0.0, 0.0, 1.0], jnp.float32)
    steps_z = jnp.array(offsets, jnp.float32) * spacing
    delta = there[:, :3, :] - here[None, :3, :] + steps_z[:, None, None] * lift[None, :, None]
    scaled = lax.optimization_barrier(jnp.sum(delta * delta, axis=1)) / cutoff_sq
    radial, slope = radial_tables(scaled)
    kinds = jnp.arange(SPECIES, dtype=jnp.float32)
    other = (there[:, 3:4, :] == kinds[None, :, None]).astype(jnp.float32)
    here_words = here[4].astype(jnp.int32)
    there_words = there[:, 4, :].astype(jnp.int32)
    upward = jnp.array([offset > 0 for offset in offsets])
    source = jnp.where(upward[:, None], here_words[None, :], there_words)
    bits = jnp.array([offset - 1 if offset > 0 else -offset - 1 for offset in offsets], jnp.int32)
    linked = jnp.bitwise_and(jnp.right_shift(source, bits[:, None]), 1).astype(jnp.float32)
    return (delta, radial, slope, other, linked)

def density(padded, atom_count):
    delta, radial, slope, other, linked = pair_tables(padded, atom_count)
    grid = jnp.einsum('ozi,oni->zni', other, radial * linked[:, None, :], precision=HIGHEST)
    return grid.reshape(SPECIES * RADIAL, atom_count)

def slope_field(field_density, own_kinds, coefs):
    channels = field_density.shape[0]
    result = jnp.zeros_like(field_density)
    for kind in range(SPECIES):
        quad = coefs[kind, :channels, :]
        part = coefs[kind, channels][:, None] + jnp.dot(quad + quad.T, field_density, precision=HIGHEST) / math.sqrt(channels)
        result = result + own_kinds[kind][None, :] * part
    return result

def pull_force(slopes, slopes_pad, padded, own_kinds, atom_count):
    delta, radial, slope, other, linked = pair_tables(padded, atom_count)
    own_grid = slopes.reshape(SPECIES, RADIAL, atom_count)
    there_slopes = shifted_stack(slopes_pad, atom_count).reshape(2 * WINDOW, SPECIES, RADIAL, atom_count)
    outward = jnp.einsum('ozi,zni->oni', other, own_grid, precision=HIGHEST)
    inward = jnp.einsum('zi,ozni->oni', own_kinds, there_slopes, precision=HIGHEST)
    strength = lax.optimization_barrier(jnp.sum((outward + inward) * slope, axis=1)) * linked * (2.0 / cutoff_sq)
    return lax.optimization_barrier(jnp.sum(strength[:, None, :] * delta, axis=0))

def back_local(field_density, values, value_pad, padded, own_kinds, atom_count):
    delta, radial, slope, other, linked = pair_tables(padded, atom_count)
    there_values = shifted_stack(value_pad, atom_count)
    project = lax.optimization_barrier(jnp.sum(delta * (values[None] - there_values), axis=1)) * linked * (2.0 / cutoff_sq)
    channels = field_density.shape[0]
    weights = jnp.einsum('ozi,oni->zni', other, slope * project[:, None, :], precision=HIGHEST).reshape(channels, atom_count)
    rows = []
    for kind in range(SPECIES):
        masked = field_density * own_kinds[kind][None, :]
        cross = jnp.dot(masked, weights.T, precision=HIGHEST)
        linear = lax.optimization_barrier(jnp.sum(weights * own_kinds[kind][None, :], axis=1))
        rows.append(jnp.concatenate([(cross + cross.T) / math.sqrt(channels), linear[None, :]], axis=0))
    return jnp.stack(rows)

def rotation(rho_bar, phi_bar, beta_norm, alpha_norm):
    rho_new = jnp.sqrt(rho_bar * rho_bar + beta_norm * beta_norm)
    cosine = rho_bar / rho_new
    sine_term = beta_norm / rho_new
    theta_term = sine_term * alpha_norm
    return (rho_new, theta_term, cosine * phi_bar, -cosine * alpha_norm, sine_term * phi_bar)

def reference(positions, species, atom_words, left_vector, right_vector, direction, solution, scalars):
    atom_count = NATOMS
    pad_edges = ((0, 0), (WINDOW, WINDOW))
    left_total = 3 * NATOMS * SNAPS
    coef_total = right_vector.size
    back_unit = force_unit * coef_total / left_total
    paddeds = []
    kinds_list = []
    densities = []
    for snapshot in range(SNAPS):
        geometry = jnp.concatenate([positions[snapshot], species[snapshot].astype(jnp.float32)[None], atom_words[snapshot].astype(jnp.float32)[None]], axis=0)
        padded = jnp.pad(geometry, pad_edges)
        own_kinds = (species[snapshot][None, :] == jnp.arange(SPECIES, dtype=jnp.int32)[:, None]).astype(jnp.float32)
        paddeds.append(padded)
        kinds_list.append(own_kinds)
        densities.append(density(padded, atom_count))
    alpha_norm = scalars[0]
    rho_bar = scalars[1]
    phi_bar = scalars[2]
    left_now = left_vector
    right_now = right_vector
    direction_now = direction
    solution_now = solution
    for sweep in range(ITERS):
        forces = []
        for snapshot in range(SNAPS):
            slopes = slope_field(densities[snapshot], kinds_list[snapshot], right_now)
            forces.append(pull_force(slopes, jnp.pad(slopes, pad_edges), paddeds[snapshot], kinds_list[snapshot], atom_count))
        left_now = force_unit * jnp.stack(forces) - alpha_norm * left_now
        beta_norm = jnp.sqrt(jnp.sum(left_now * left_now) / left_total + tiny)
        left_now = left_now / beta_norm
        totals = jnp.zeros_like(right_now)
        for snapshot in range(SNAPS):
            totals = totals + back_local(densities[snapshot], left_now[snapshot], jnp.pad(left_now[snapshot], pad_edges), paddeds[snapshot], kinds_list[snapshot], atom_count)
        right_now = back_unit * totals - beta_norm * right_now
        alpha_norm = jnp.sqrt(jnp.sum(right_now * right_now) / coef_total + tiny)
        right_now = right_now / alpha_norm
        rho_new, theta_term, phi_term, rho_bar, phi_bar = rotation(rho_bar, phi_bar, beta_norm, alpha_norm)
        solution_now = solution_now + phi_term / rho_new * direction_now
        direction_now = right_now - theta_term / rho_new * direction_now
    return (left_now, right_now, direction_now, solution_now, jnp.stack([alpha_norm, rho_bar, phi_bar]))
```

```python
import functools
import math

import jax
import jax.numpy as jnp
from jax import lax
from jax.experimental import pallas as pl
from jax.experimental.pallas import tpu as pltpu
from jax.sharding import PartitionSpec as P

SPECIES = 5
RADIAL = 16
WINDOW = 15
ITERS = 3
CHANNELS = SPECIES * RADIAL
BLOCK = 88
HALF = CHANNELS // 2
ROWS = 256
LANES = 128
HALO = 64

cutoff_sq = 36.0
spacing = 0.25
force_unit = 0.015625
tiny = 1e-06
HIGHEST = lax.Precision.HIGHEST
MESH = pl.DeviceIdType.MESH


def turn(x, shift):
    width = x.shape[1]
    return pltpu.roll(x, shift % width, 1)


def row_sum(x):
    return jnp.sum(x, axis=0, keepdims=True)


def prepare(cells_ref, psi_ref, delta_ref, near_ref, masked_ref, own_ref, phi_ref, scaled_ref):
    width = cells_ref.shape[1]
    here = cells_ref[...]
    row_id = lax.broadcasted_iota(jnp.int32, (8, width), 0)
    near_ref[...] = jnp.full(near_ref.shape, -1.0, jnp.float32)
    scaled_ref[...] = jnp.ones(scaled_ref.shape, jnp.float32)
    for o in range(1, WINDOW + 1):
        there = turn(here, -o)
        delta = there - here + jnp.where(row_id == 2, spacing * o, 0.0)
        delta = jnp.where(row_id < 3, delta, 0.0)
        delta_ref[o - 1] = delta
        scaled_ref[o - 1 : o, :] = row_sum(delta * delta)
        near_ref[0, o - 1 : o, :] = there[3:4, :]
        near_ref[1, o - 1 : o, :] = turn(here, o)[3:4, :]
    scaled = scaled_ref[...] / cutoff_sq
    words = jnp.broadcast_to(here[4:5, :].astype(jnp.int32), scaled.shape)
    bits = lax.broadcasted_iota(jnp.int32, scaled.shape, 0)
    linked = jnp.bitwise_and(jnp.right_shift(words, bits), 1).astype(jnp.float32)
    envelope = jnp.maximum(1.0 - scaled, 0.0)
    argument = 2.0 * jnp.minimum(scaled, 1.0) - 1.0
    twice = 2.0 * argument
    square = envelope * envelope * linked
    line = -2.0 * envelope * linked
    first = [jnp.ones_like(argument), argument]
    second = [jnp.ones_like(argument), twice]
    for n in range(RADIAL):
        if n >= 2:
            first.append(twice * first[-1] - first[-2])
            second.append(twice * second[-1] - second[-2])
        damping = 1.0 / (1.0 + n)
        phi = square * first[n] * damping
        psi = line * first[n]
        if n > 0:
            psi = psi + 2.0 * n * square * second[n - 1]
        phi_ref[0, :, n, :] = phi
        psi_ref[0, :, n, :] = psi * damping
    for o in range(1, WINDOW + 1):
        phi_ref[1, o - 1] = turn(phi_ref[0, o - 1], o)
        psi_ref[1, o - 1] = turn(psi_ref[0, o - 1], o)
    kinds = here[3:4, :]
    own_ref[...] = jnp.where(
        jnp.broadcast_to(kinds, (8, width)) == row_id.astype(jnp.float32), 1.0, 0.0
    )
    for tile in range(width // LANES):
        at = slice(tile * LANES, (tile + 1) * LANES)
        sums = [jnp.zeros((RADIAL, LANES), jnp.float32) for _ in range(SPECIES)]
        for side in range(2):
            for o in range(WINDOW):
                value = phi_ref[side, o, :, at]
                kind = jnp.broadcast_to(near_ref[side, o : o + 1, at], (RADIAL, LANES))
                for c in range(SPECIES):
                    sums[c] = sums[c] + jnp.where(kind == c, value, 0.0)
        first_row = lax.broadcasted_iota(jnp.int32, (8, LANES), 0) == 0
        for z in range(SPECIES):
            own = own_ref[z : z + 1, at]
            for c in range(SPECIES):
                start = z * BLOCK + c * RADIAL
                masked_ref[start : start + RADIAL, at] = jnp.where(own > 0.5, sums[c], 0.0)
                if z == 0:
                    phi_ref[0, c, :, at] = sums[c]
            start = z * BLOCK + CHANNELS
            masked_ref[start : start + 8, at] = jnp.where(
                first_row, jnp.broadcast_to(own, (8, LANES)), 0.0
            )


def advance(total_ref, sums, state):
    v_in, pair_in, w_in, x_in, sc_in, raw_in = state
    left_total, coef_total = sums
    back_unit = force_unit * coef_total / left_total
    rho_bar = sc_in[1:2, 0:1]
    phi_bar = sc_in[2:3, 0:1]
    beta = jnp.sqrt(total_ref[ROWS - 8 : ROWS - 7, 0:1] / left_total + tiny)
    scale = back_unit / beta
    root = 1.0 / math.sqrt(CHANNELS)
    lane = lax.broadcasted_iota(jnp.int32, (HALF, LANES), 1)
    backs = []
    for z in range(SPECIES):
        packed = total_ref[z * HALF : (z + 1) * HALF, :]
        square = jnp.concatenate(
            [packed, jnp.zeros((LANES - HALF, LANES), jnp.float32)], axis=0
        )
        flipped = square.T[HALF:CHANNELS, :]
        lower = jnp.where(lane < HALF, flipped, turn(packed, -HALF))
        quad = jnp.concatenate([packed[:, :CHANNELS], lower[:, :CHANNELS]], axis=0) * root
        start = SPECIES * HALF + z
        backs.append((quad, total_ref[start : start + 1, :CHANNELS]))
    raws = []
    power = jnp.zeros((1, 1), jnp.float32)
    for z in range(SPECIES):
        quad = scale * backs[z][0] - beta * v_in[z, :CHANNELS, :]
        line = scale * backs[z][1] - beta * v_in[z, CHANNELS : CHANNELS + 1, :]
        raws.append((quad, line))
        power = power + jnp.sum(jnp.sum(quad * quad, axis=0, keepdims=True) + line * line,
                                axis=1, keepdims=True)
    alpha = jnp.sqrt(power / coef_total + tiny)
    rho = jnp.sqrt(rho_bar * rho_bar + beta * beta)
    cosine = rho_bar / rho
    sine = beta / rho
    theta = sine * alpha
    phi = cosine * phi_bar
    scalars = (alpha, -cosine * alpha, sine * phi_bar)
    inverse = 1.0 / alpha
    vs, pairs, ws, xs = [], [], [], []
    for z in range(SPECIES):
        quad = raws[z][0] * inverse
        line = raws[z][1] * inverse
        v = jnp.concatenate([quad, line], axis=0)
        w = w_in[z]
        vs.append(v)
        xs.append(x_in[z] + (phi / rho) * w)
        ws.append(v - (theta / rho) * w)
        old = pair_in[z * BLOCK : z * BLOCK + CHANNELS, :]
        pairs.append((2.0 * root * scale * backs[z][0] - beta * old) * inverse)
    left = raw_in[...] / beta
    return vs, pairs, ws, xs, scalars, left


def write_scalars(ref, scalars):
    row_id = lax.broadcasted_iota(jnp.int32, ref.shape, 0)
    ref[...] = jnp.where(row_id == 0, scalars[0], jnp.where(row_id == 1, scalars[1], scalars[2]))


def sweep(own_count, alpha, left, pair_ref, psi_ref, delta_ref, near_ref, masked_ref, own_ref,
          density, raw_ref, out_ref, slope_ref, pull_ref, weight_ref, rhs_ref, lhs_ref):
    width = masked_ref.shape[1]
    unit = 2.0 / cutoff_sq
    slope_ref[...] = lax.dot_general(
        pair_ref[...], masked_ref[...], (((0,), (0,)), ((), ())),
        precision=HIGHEST, preferred_element_type=jnp.float32,
    )
    for tile in range(width // LANES):
        at = slice(tile * LANES, (tile + 1) * LANES)
        parts = [slope_ref[c * RADIAL : (c + 1) * RADIAL, at] for c in range(SPECIES)]
        for side in range(2):
            for o in range(WINDOW):
                kind = jnp.broadcast_to(near_ref[side, o : o + 1, at], (RADIAL, LANES))
                chosen = parts[0]
                for c in range(1, SPECIES):
                    chosen = jnp.where(kind == c, parts[c], chosen)
                pull_ref[side, o : o + 1, at] = row_sum(chosen * psi_ref[side, o, :, at])
    force = jnp.zeros((8, width), jnp.float32)
    for o in range(1, WINDOW + 1):
        pull = pull_ref[0, o - 1 : o, :] + turn(pull_ref[1, o - 1 : o, :], -o)
        term = (unit * pull) * delta_ref[o - 1]
        force = force + term - turn(term, o)
    raw = force_unit * force - alpha * left
    raw_ref[...] = raw
    for o in range(1, WINDOW + 1):
        project = unit * row_sum(delta_ref[o - 1] * (raw - turn(raw, -o)))
        pull_ref[0, o - 1 : o, :] = project
        pull_ref[1, o - 1 : o, :] = turn(project, o)
    for tile in range(own_count // LANES):
        at = slice(tile * LANES, (tile + 1) * LANES)
        behind = slice(own_count + tile * LANES, own_count + (tile + 1) * LANES)
        sums = [jnp.zeros((RADIAL, LANES), jnp.float32) for _ in range(SPECIES)]
        for side in range(2):
            for o in range(WINDOW):
                value = psi_ref[side, o, :, at] * pull_ref[side, o : o + 1, at]
                kind = jnp.broadcast_to(near_ref[side, o : o + 1, at], (RADIAL, LANES))
                for c in range(SPECIES):
                    sums[c] = sums[c] + jnp.where(kind == c, value, 0.0)
        for c in range(SPECIES):
            rhs_ref[c * RADIAL : (c + 1) * RADIAL, at] = sums[c]
            rhs_ref[c * RADIAL : (c + 1) * RADIAL, behind] = density(c, at)
        rhs_ref[CHANNELS:, at] = jnp.zeros((LANES - CHANNELS, LANES), jnp.float32)
        rhs_ref[CHANNELS:, behind] = jnp.zeros((LANES - CHANNELS, LANES), jnp.float32)
        for z in range(SPECIES):
            own = own_ref[z : z + 1, at]
            for c in range(SPECIES):
                start = z * BLOCK + c * RADIAL
                lhs_ref[start : start + RADIAL, behind] = jnp.where(own > 0.5, sums[c], 0.0)
            start = z * BLOCK + CHANNELS
            lhs_ref[start : start + 8, behind] = jnp.zeros((8, LANES), jnp.float32)
        lhs_ref[:, at] = masked_ref[:, at]
    cross = lax.dot_general(
        lhs_ref[...], rhs_ref[...], (((1,), (1,)), ((), ())),
        precision=HIGHEST, preferred_element_type=jnp.float32,
    )
    lane = lax.broadcasted_iota(jnp.int32, (HALF, LANES), 1)
    out_ref[SPECIES * HALF :, :] = jnp.zeros((ROWS - SPECIES * HALF, LANES), jnp.float32)
    for z in range(SPECIES):
        upper = cross[z * BLOCK : z * BLOCK + HALF, :]
        lower = cross[z * BLOCK + HALF : z * BLOCK + CHANNELS, :]
        out_ref[z * HALF : (z + 1) * HALF, :] = jnp.where(lane < CHANNELS, upper, turn(lower, HALF))
        start = SPECIES * HALF + z
        out_ref[start : start + 1, :] = cross[z * BLOCK + CHANNELS : z * BLOCK + CHANNELS + 1, :]
    mine = raw[:, :own_count]
    square = jnp.sum(row_sum(mine * mine), axis=1, keepdims=True)
    out_ref[ROWS - 8 : ROWS, :] = jnp.broadcast_to(square, (8, LANES))


def first_kernel(own_count, cells_ref, sc_ref, pair_ref,
                 psi_ref, delta_ref, near_ref, masked_ref, own_ref, dens_ref, raw_ref, out_ref,
                 phi_ref, scaled_ref, *scratch):
    prepare(cells_ref, psi_ref, delta_ref, near_ref, masked_ref, own_ref, phi_ref, scaled_ref)
    dens_ref[...] = phi_ref[0, :SPECIES]
    cells = cells_ref[...]
    left = jnp.concatenate([cells[5:8], jnp.zeros((5, cells.shape[1]), jnp.float32)], axis=0)
    sweep(own_count, sc_ref[0:1, 0:1], left, pair_ref, psi_ref, delta_ref, near_ref, masked_ref,
          own_ref, lambda c, at: dens_ref[c, :, at], raw_ref, out_ref, *scratch)


def middle_kernel(own_count, sums, total_ref, v_in, pair_in, w_in, x_in, sc_in, raw_in,
                  psi_ref, delta_ref, near_ref, masked_ref, own_ref, dens_ref,
                  v_ref, pair_ref, w_ref, x_ref, sc_ref, raw_ref, out_ref, *scratch):
    vs, pairs, ws, xs, scalars, left = advance(
        total_ref, sums, (v_in, pair_in, w_in, x_in, sc_in, raw_in))
    for z in range(SPECIES):
        v_ref[z] = vs[z]
        w_ref[z] = ws[z]
        x_ref[z] = xs[z]
        start = z * BLOCK
        pair_ref[start : start + CHANNELS, :] = pairs[z]
        pair_ref[start + CHANNELS : start + BLOCK, :] = jnp.zeros(
            (BLOCK - CHANNELS, CHANNELS), jnp.float32)
        pair_ref[start + CHANNELS : start + CHANNELS + 1, :] = vs[z][CHANNELS:]
    write_scalars(sc_ref, scalars)
    sweep(own_count, scalars[0], left, pair_ref, psi_ref, delta_ref, near_ref, masked_ref,
          own_ref, lambda c, at: dens_ref[c, :, at], raw_ref, out_ref, *scratch)


def last_kernel(sums, total_ref, v_in, pair_in, w_in, x_in, sc_in, raw_in,
                v_ref, w_ref, x_ref, sc_ref, left_ref):
    vs, _, ws, xs, scalars, left = advance(
        total_ref, sums, (v_in, pair_in, w_in, x_in, sc_in, raw_in))
    for z in range(SPECIES):
        v_ref[z] = vs[z]
        w_ref[z] = ws[z]
        x_ref[z] = xs[z]
    write_scalars(sc_ref, scalars)
    left_ref[...] = left[0:3, : left_ref.shape[1]]


def reduce_kernel(n_snap, n_brick, x_ref, o_ref, slots, full, send_a, recv_a, send_b, recv_b):
    count = n_snap * n_brick
    owners = min(count, ROWS // 8)
    stride = count // owners
    rows = ROWS // owners
    me = lax.axis_index("snap") * n_brick + lax.axis_index("brick")
    barrier = pltpu.get_barrier_semaphore()

    def device(p):
        return (p // n_brick, lax.rem(p, n_brick))

    def every_owner(act):
        if stride == 1:
            def body(k, carry):
                act(lax.rem(me + k, count))
                return carry
            lax.fori_loop(1, count, body, 0)
        else:
            def body(k, carry):
                p = lax.rem(me // stride + k, owners) * stride

                @pl.when(p != me)
                def _():
                    act(p)
                return carry
            lax.fori_loop(0, owners, body, 0)

    def everyone(act):
        def body(k, carry):
            act(lax.rem(me + k, count))
            return carry
        lax.fori_loop(1, count, body, 0)

    def when_owner(yes, no):
        if stride == 1:
            yes()
        else:
            pl.when(lax.rem(me, stride) == 0)(yes)
            pl.when(lax.rem(me, stride) != 0)(no)

    def greet(p):
        pl.semaphore_signal(barrier, inc=1, device_id=device(p), device_id_type=MESH)

    def greet_all():
        everyone(greet)
        pl.semaphore_wait(barrier, count - 1)

    def greet_owners():
        every_owner(greet)
        pl.semaphore_wait(barrier, owners)

    when_owner(greet_all, greet_owners)

    def chunk(ref, p):
        return ref.at[pl.ds(pl.multiple_of((p // stride) * rows, rows), rows), :]

    def send_part(p):
        pltpu.make_async_remote_copy(
            src_ref=chunk(x_ref, p), dst_ref=slots.at[me], send_sem=send_a, recv_sem=recv_a,
            device_id=device(p), device_id_type=MESH,
        ).start()

    def bytes_of(amount, sem):
        view = full.at[pl.ds(0, amount * rows), :]
        pltpu.make_async_copy(view, view, sem).wait()

    def gather_slots(amount, sem):
        view = slots.at[pl.ds(0, amount)]
        pltpu.make_async_copy(view, view, sem).wait()

    every_owner(send_part)

    def finish_owner():
        mine = pl.multiple_of((me // stride) * rows, rows)
        slots[me] = x_ref[pl.ds(mine, rows), :]
        gather_slots(count - 1, recv_a)
        total = slots[0]
        for p in range(1, count):
            total = total + slots[p]
        full[pl.ds(mine, rows), :] = total

        def send_sum(p):
            pltpu.make_async_remote_copy(
                src_ref=chunk(full, me), dst_ref=chunk(full, me), send_sem=send_b,
                recv_sem=recv_b, device_id=device(p), device_id_type=MESH,
            ).start()

        everyone(send_sum)
        bytes_of(owners - 1, send_a)
        bytes_of(owners - 1, recv_b)
        gather_slots(count - 1, send_b)

    def finish_other():
        bytes_of(owners, send_a)
        bytes_of(owners, recv_b)

    when_owner(finish_owner, finish_other)
    o_ref[...] = full[...]


def shards(n_snap, n_brick, positions, species, atom_words, left_vector, right_vector, direction,
           solution_in, scalars):
    own_count = positions.shape[2]
    width = own_count + 2 * HALO
    coef_total = float(right_vector.size)
    left_total = float(3 * own_count * n_snap * n_brick * positions.shape[0])
    sums = (left_total, coef_total)
    f32 = jnp.float32

    own = jnp.concatenate(
        [positions[0], species.astype(f32), atom_words.astype(f32), left_vector[0]], axis=0)
    right = lax.ppermute(own[:, :HALO], "brick", [(i + 1, i) for i in range(n_brick - 1)])
    left = lax.ppermute(own[:, -HALO:], "brick", [(i, i + 1) for i in range(n_brick - 1)])
    cells = jnp.concatenate([own, right, left], axis=1)

    quad = right_vector[:, :CHANNELS, :]
    pair = (quad + jnp.swapaxes(quad, 1, 2)) / math.sqrt(CHANNELS)
    pair = jnp.concatenate(
        [pair, right_vector[:, CHANNELS:, :],
         jnp.zeros((SPECIES, BLOCK - CHANNELS - 1, CHANNELS), f32)], axis=1
    ).reshape(SPECIES * BLOCK, CHANNELS)
    sc = jnp.broadcast_to(jnp.pad(scalars, (0, 5))[:, None], (8, LANES))

    def shape(*dims):
        return jax.ShapeDtypeStruct(dims, f32)

    vmem = pl.BlockSpec(memory_space=pltpu.VMEM)
    params = pltpu.CompilerParams(vmem_limit_bytes=32 * 2**20)
    tables = [
        shape(2, 16, RADIAL, width), shape(16, 8, width), shape(2, 16, width),
        shape(SPECIES * BLOCK, width), shape(8, width), shape(SPECIES, RADIAL, width),
    ]
    coefs = shape(SPECIES, CHANNELS + 1, CHANNELS)
    pairs = shape(SPECIES * BLOCK, CHANNELS)
    raws = shape(8, width)
    message = shape(ROWS, LANES)
    work = [
        pltpu.VMEM((CHANNELS, width), f32), pltpu.VMEM((2, 16, width), f32),
        pltpu.VMEM((8, LANES), f32), pltpu.VMEM((LANES, 2 * own_count), f32),
        pltpu.VMEM((SPECIES * BLOCK, 2 * own_count), f32),
    ]

    def call(body, inputs, outs, scratch):
        return pl.pallas_call(
            body, out_shape=outs, in_specs=[vmem] * len(inputs), out_specs=[vmem] * len(outs),
            scratch_shapes=scratch, compiler_params=params,
        )(*inputs)

    count = n_snap * n_brick
    owners = min(count, ROWS // 8)

    def total(part):
        return pl.pallas_call(
            functools.partial(reduce_kernel, n_snap, n_brick),
            out_shape=message, in_specs=[vmem], out_specs=vmem,
            scratch_shapes=[
                pltpu.VMEM((count, ROWS // owners, LANES), f32), pltpu.VMEM((ROWS, LANES), f32),
            ] + [pltpu.SemaphoreType.DMA] * 4,
            compiler_params=pltpu.CompilerParams(collective_id=0, has_side_effects=True),
        )(part)

    *kept, raw, part = call(
        functools.partial(first_kernel, own_count), [cells, sc, pair], tables + [raws, message],
        [pltpu.VMEM((2, 16, RADIAL, width), f32), pltpu.VMEM((16, width), f32)] + work)
    v, w, x = right_vector, direction, solution_in
    for _ in range(ITERS - 1):
        v, pair, w, x, sc, raw, part = call(
            functools.partial(middle_kernel, own_count, sums),
            [total(part), v, pair, w, x, sc, raw] + kept,
            [coefs, pairs, coefs, coefs, shape(8, LANES), raws, message], work)
    v, w, x, sc, left_next = call(
        functools.partial(last_kernel, sums), [total(part), v, pair, w, x, sc, raw],
        [coefs, coefs, coefs, shape(8, LANES), shape(3, own_count)], [])
    return (left_next[None], v, w, x, sc[:3, 0])


def solution(mesh):
    placed = (
        P("snap", None, "brick"), P("snap", "brick"), P("snap", "brick"),
        P("snap", None, "brick"), P(), P(), P(), P(),
    )
    return jax.shard_map(
        functools.partial(shards, mesh.shape["snap"], mesh.shape["brick"]),
        mesh=mesh, in_specs=placed,
        out_specs=(P("snap", None, "brick"), P(), P(), P(), P()), check_vma=False,
    )
```

```python
import functools
import math

import jax
import jax.numpy as jnp
from jax import lax
from jax.experimental import pallas as pl
from jax.experimental.pallas import tpu as pltpu
from jax.sharding import PartitionSpec as P

SPECIES = 5
RADIAL = 16
WINDOW = 15
ITERS = 3
CHANNELS = SPECIES * RADIAL
BLOCK = 128
HALF = CHANNELS // 2
TERMS = CHANNELS + 1
MOVE = 128 - TERMS
ROWS = 256
LANES = 128
HALO = 64

cutoff_sq = 36.0
spacing = 0.25
force_unit = 0.015625
tiny = 1e-06
HIGHEST = lax.Precision.HIGHEST
MESH = pl.DeviceIdType.MESH


def turn(x, shift):
    width = x.shape[1]
    return pltpu.roll(x, shift % width, 1)


def row_sum(x):
    return jnp.sum(x, axis=0, keepdims=True)


def prepare(cells_ref, psi_ref, delta_ref, near_ref, masked_ref, own_ref, dens_ref, phi_ref,
            scaled_ref):
    width = cells_ref.shape[1]
    here = cells_ref[...]
    row_id = lax.broadcasted_iota(jnp.int32, (8, width), 0)
    near_ref[...] = jnp.full(near_ref.shape, -1.0, jnp.float32)
    scaled_ref[...] = jnp.ones(scaled_ref.shape, jnp.float32)
    for o in range(1, WINDOW + 1):
        there = turn(here, -o)
        delta = there - here + jnp.where(row_id == 2, spacing * o, 0.0)
        delta = jnp.where(row_id < 3, delta, 0.0)
        delta_ref[o - 1] = delta
        scaled_ref[o - 1 : o, :] = row_sum(delta * delta)
        near_ref[0, o - 1 : o, :] = there[3:4, :]
        near_ref[1, o - 1 : o, :] = turn(here, o)[3:4, :]
    scaled = scaled_ref[...] / cutoff_sq
    words = jnp.broadcast_to(here[4:5, :].astype(jnp.int32), scaled.shape)
    bits = lax.broadcasted_iota(jnp.int32, scaled.shape, 0)
    linked = jnp.bitwise_and(jnp.right_shift(words, bits), 1).astype(jnp.float32)
    envelope = jnp.maximum(1.0 - scaled, 0.0)
    argument = 2.0 * jnp.minimum(scaled, 1.0) - 1.0
    twice = 2.0 * argument
    square = envelope * envelope * linked
    line = -2.0 * envelope * linked
    first = [jnp.ones_like(argument), argument]
    second = [jnp.ones_like(argument), twice]
    for n in range(RADIAL):
        if n >= 2:
            first.append(twice * first[-1] - first[-2])
            second.append(twice * second[-1] - second[-2])
        damping = 1.0 / (1.0 + n)
        phi = square * first[n] * damping
        psi = line * first[n]
        if n > 0:
            psi = psi + 2.0 * n * square * second[n - 1]
        phi_ref[0, :, n, :] = phi
        psi_ref[0, :, n, :] = psi * damping
    for o in range(1, WINDOW + 1):
        phi_ref[1, o - 1] = turn(phi_ref[0, o - 1], o)
        psi_ref[1, o - 1] = turn(psi_ref[0, o - 1], o)
    kinds = here[3:4, :]
    own_ref[...] = jnp.where(
        jnp.broadcast_to(kinds, (8, width)) == row_id.astype(jnp.float32), 1.0, 0.0
    )
    masked_ref[...] = jnp.zeros(masked_ref.shape, jnp.float32)
    for tile in range(width // LANES):
        at = slice(tile * LANES, (tile + 1) * LANES)
        sums = [jnp.zeros((RADIAL, LANES), jnp.float32) for _ in range(SPECIES)]
        for side in range(2):
            for o in range(WINDOW):
                value = phi_ref[side, o, :, at]
                kind = jnp.broadcast_to(near_ref[side, o : o + 1, at], (RADIAL, LANES))
                for c in range(SPECIES):
                    sums[c] = sums[c] + jnp.where(kind == c, value, 0.0)
        first_row = lax.broadcasted_iota(jnp.int32, (8, LANES), 0) == 0
        for z in range(SPECIES):
            own = own_ref[z : z + 1, at]
            for c in range(SPECIES):
                start = z * BLOCK + c * RADIAL
                masked_ref[start : start + RADIAL, at] = jnp.where(own > 0.5, sums[c], 0.0)
                if z == 0:
                    dens_ref[c * RADIAL : (c + 1) * RADIAL, at] = sums[c]
            start = z * BLOCK + CHANNELS
            masked_ref[start : start + 8, at] = jnp.where(
                first_row, jnp.broadcast_to(own, (8, LANES)), 0.0
            )


def advance(total, sums, v_ref, w_ref, x_ref, pair_ref, sc_ref, raw_ref):
    left_total, coef_total = sums
    back_unit = force_unit * coef_total / left_total
    rho_bar = sc_ref[1:2, 0:1]
    phi_bar = sc_ref[2:3, 0:1]
    beta = jnp.sqrt(total(0)[0:1, TERMS : TERMS + 1] / left_total + tiny)
    scale = back_unit / beta
    lane = lax.broadcasted_iota(jnp.int32, (HALF, LANES), 1)
    wide = lax.broadcasted_iota(jnp.int32, (CHANNELS, LANES), 1)
    last = jnp.where(wide == CHANNELS, 1.0, 0.0)
    once = jnp.where(wide < CHANNELS, 1.0 / math.sqrt(CHANNELS), last) * scale
    twice = jnp.where(wide < CHANNELS, 2.0 / CHANNELS, last) * scale
    power = jnp.zeros((1, TERMS), jnp.float32)
    for z in range(SPECIES):
        at = slice(z * BLOCK, (z + 1) * BLOCK)
        packed = total(z)
        square = jnp.concatenate(
            [packed, jnp.zeros((LANES - HALF, LANES), jnp.float32)], axis=0
        )
        lower = jnp.where(lane < HALF, square.T[HALF:CHANNELS, :], turn(packed, -MOVE))
        back = jnp.concatenate([packed, lower], axis=0)
        v = (once * back)[:, :TERMS] - beta * v_ref[z]
        v_ref[z] = v
        power = power + row_sum(v * v)
        pair_ref[:, at] = twice * back - beta * pair_ref[:, at]
    alpha = jnp.sqrt(jnp.sum(power, axis=1, keepdims=True) / coef_total + tiny)
    rho = jnp.sqrt(rho_bar * rho_bar + beta * beta)
    cosine = rho_bar / rho
    sine = beta / rho
    theta = sine * alpha
    phi = cosine * phi_bar
    inverse = 1.0 / alpha
    for z in range(SPECIES):
        at = slice(z * BLOCK, (z + 1) * BLOCK)
        v = v_ref[z] * inverse
        v_ref[z] = v
        w = w_ref[z]
        x_ref[z] = x_ref[z] + (phi / rho) * w
        w_ref[z] = v - (theta / rho) * w
        pair_ref[:, at] = pair_ref[:, at] * inverse
    raw_ref[...] = raw_ref[...] / beta
    write_scalars(sc_ref, alpha, -cosine * alpha, sine * phi_bar)


def write_scalars(ref, alpha, rho_bar, phi_bar):
    row_id = lax.broadcasted_iota(jnp.int32, ref.shape, 0)
    ref[...] = jnp.where(row_id == 0, alpha, jnp.where(row_id == 1, rho_bar, phi_bar))


def sweep(own_count, alpha, left, pair_ref, psi_ref, delta_ref, near_ref, masked_ref, own_ref,
          raw_ref, out_ref, slope_ref, pull_ref, rhs_ref, lhs_ref):
    width = masked_ref.shape[1]
    unit = 2.0 / cutoff_sq
    slope_ref[...] = jnp.dot(
        pair_ref[...], masked_ref[...], precision=HIGHEST, preferred_element_type=jnp.float32
    )
    for tile in range(width // LANES):
        at = slice(tile * LANES, (tile + 1) * LANES)
        parts = [slope_ref[c * RADIAL : (c + 1) * RADIAL, at] for c in range(SPECIES)]
        for side in range(2):
            for o in range(WINDOW):
                kind = jnp.broadcast_to(near_ref[side, o : o + 1, at], (RADIAL, LANES))
                chosen = parts[0]
                for c in range(1, SPECIES):
                    chosen = jnp.where(kind == c, parts[c], chosen)
                pull_ref[side, o : o + 1, at] = row_sum(chosen * psi_ref[side, o, :, at])
    force = jnp.zeros((8, width), jnp.float32)
    for o in range(1, WINDOW + 1):
        pull = pull_ref[0, o - 1 : o, :] + turn(pull_ref[1, o - 1 : o, :], -o)
        term = (unit * pull) * delta_ref[o - 1]
        force = force + term - turn(term, o)
    raw = force_unit * force - alpha * left
    raw_ref[...] = raw
    for o in range(1, WINDOW + 1):
        project = unit * row_sum(delta_ref[o - 1] * (raw - turn(raw, -o)))
        pull_ref[0, o - 1 : o, :] = project
        pull_ref[1, o - 1 : o, :] = turn(project, o)
    for tile in range(own_count // LANES):
        at = slice(tile * LANES, (tile + 1) * LANES)
        behind = slice(own_count + tile * LANES, own_count + (tile + 1) * LANES)
        sums = [jnp.zeros((RADIAL, LANES), jnp.float32) for _ in range(SPECIES)]
        for side in range(2):
            for o in range(WINDOW):
                value = psi_ref[side, o, :, at] * pull_ref[side, o : o + 1, at]
                kind = jnp.broadcast_to(near_ref[side, o : o + 1, at], (RADIAL, LANES))
                for c in range(SPECIES):
                    sums[c] = sums[c] + jnp.where(kind == c, value, 0.0)
        for c in range(SPECIES):
            rhs_ref[c * RADIAL : (c + 1) * RADIAL, at] = sums[c]
        for z in range(SPECIES):
            own = own_ref[z : z + 1, at]
            for c in range(SPECIES):
                start = z * BLOCK + c * RADIAL
                lhs_ref[start : start + RADIAL, behind] = jnp.where(own > 0.5, sums[c], 0.0)
    cross = lax.dot_general(
        rhs_ref[...], lhs_ref[...], (((1,), (1,)), ((), ())),
        precision=HIGHEST, preferred_element_type=jnp.float32,
    )
    lane = lax.broadcasted_iota(jnp.int32, (HALF, LANES), 1)
    mine = raw[:, :own_count]
    square = jnp.sum(row_sum(mine * mine), axis=1, keepdims=True)
    for z in range(SPECIES):
        block = cross[:, z * BLOCK : (z + 1) * BLOCK]
        upper = jnp.where(lane == TERMS, square, block[:HALF])
        out_ref[z * HALF : (z + 1) * HALF, :] = jnp.where(
            lane < HALF + MOVE, upper, turn(block[HALF:], MOVE))


def kernel(n_snap, n_brick, own_count, sums,
           pos_in, species_in, words_in, left_in, v_in, w_in, x_in, sc_in,
           left_out, v_ref, w_ref, x_ref, sc_out,
           own_ref, ends, cells_ref, psi_ref, delta_ref, near_ref, masked_ref, kinds_ref, dens_ref,
           phi_ref, scaled_ref, pair_ref, sc_ref, raw_ref, slope_ref, pull_ref, rhs_ref, lhs_ref,
           part, slots, full, halo_send, halo_recv, send_a, recv_a, send_b, recv_b):
    count = n_snap * n_brick
    owners = min(count, ROWS // 8)
    stride = count // owners
    rows = ROWS // owners
    snap = lax.axis_index("snap")
    brick = lax.axis_index("brick")
    me = snap * n_brick + brick
    barrier = pltpu.get_barrier_semaphore()

    def device(p):
        return (p // n_brick, lax.rem(p, n_brick))

    def everyone(act):
        def body(k, carry):
            act(lax.rem(me + k, count))
            return carry
        lax.fori_loop(1, count, body, 0)

    def every_owner(act):
        if stride == 1:
            everyone(act)
        else:
            def body(k, carry):
                p = lax.rem(me // stride + k, owners) * stride

                @pl.when(p != me)
                def _():
                    act(p)
                return carry
            lax.fori_loop(0, owners, body, 0)

    def when_owner(yes, no):
        if stride == 1:
            yes()
        else:
            pl.when(lax.rem(me, stride) == 0)(yes)
            pl.when(lax.rem(me, stride) != 0)(no)

    everyone(lambda p: pl.semaphore_signal(
        barrier, inc=1, device_id=device(p), device_id_type=MESH))

    for k in range(3):
        own_ref[k : k + 1, :] = pos_in[k]
        own_ref[5 + k : 6 + k, :] = left_in[k]
    own_ref[3:4, :] = species_in[...].astype(jnp.float32)
    own_ref[4:5, :] = words_in[...].astype(jnp.float32)
    pl.semaphore_wait(barrier, count - 1)

    def shift(step, source, slot):
        return pltpu.make_async_remote_copy(
            src_ref=own_ref.at[:, pl.ds(source, LANES)], dst_ref=ends.at[slot],
            send_sem=halo_send.at[slot], recv_sem=halo_recv.at[slot],
            device_id=(snap, lax.rem(brick + step + n_brick, n_brick)), device_id_type=MESH,
        )

    to_left = shift(-1, 0, 0)
    to_right = shift(1, own_count - LANES, 1)
    has_left = brick > 0
    has_right = brick < n_brick - 1
    pl.when(has_left)(to_left.start)
    pl.when(has_right)(to_right.start)

    write_scalars(sc_ref, sc_in[0], sc_in[1], sc_in[2])
    rhs_ref[...] = jnp.zeros(rhs_ref.shape, jnp.float32)
    lhs_ref[...] = jnp.zeros(lhs_ref.shape, jnp.float32)
    fill = jnp.zeros((CHANNELS, LANES - TERMS), jnp.float32)
    wide = lax.broadcasted_iota(jnp.int32, (CHANNELS, LANES), 1)
    for z in range(SPECIES):
        v = v_in[z]
        v_ref[z] = v
        w_ref[z] = w_in[z]
        x_ref[z] = x_in[z]
        padded = jnp.concatenate([v, fill], axis=1)
        tall = jnp.concatenate([padded, jnp.zeros((LANES - CHANNELS, LANES), jnp.float32)], axis=0)
        pair = (padded + tall.T[:CHANNELS, :]) * (1.0 / math.sqrt(CHANNELS))
        pair_ref[:, z * BLOCK : (z + 1) * BLOCK] = jnp.where(wide < CHANNELS, pair, padded)

    @pl.when(has_left)
    def _():
        to_left.wait_send()
        to_right.wait_recv()

    @pl.when(has_right)
    def _():
        to_right.wait_send()
        to_left.wait_recv()

    zero = jnp.zeros((8, LANES), jnp.float32)

    @pl.when(jnp.logical_not(has_left))
    def _():
        ends[1] = zero

    @pl.when(jnp.logical_not(has_right))
    def _():
        ends[0] = zero

    cells_ref[:, :own_count] = own_ref[...]
    lane = lax.broadcasted_iota(jnp.int32, (8, LANES), 1)
    cells_ref[:, own_count:] = jnp.where(lane < HALO, ends[0], ends[1])
    prepare(cells_ref, psi_ref, delta_ref, near_ref, masked_ref, kinds_ref, dens_ref, phi_ref,
            scaled_ref)
    raw_ref[...] = jnp.zeros(raw_ref.shape, jnp.float32)
    raw_ref[0:3, :] = cells_ref[5:8, :]
    lhs_ref[:, :own_count] = masked_ref[:, :own_count]
    rhs_ref[:, own_count:] = dens_ref[:, :own_count]

    def chunk(ref, i, p):
        return ref.at[i, pl.ds(pl.multiple_of((p // stride) * rows, rows), rows), :]

    def reduce(i):
        def settle(ref, amount, sem):
            view = ref.at[i, pl.ds(0, amount)]
            pltpu.make_async_copy(view, view, sem.at[i]).wait()

        def send_part(p):
            pltpu.make_async_remote_copy(
                src_ref=chunk(part, i, p), dst_ref=slots.at[i, me], send_sem=send_a.at[i],
                recv_sem=recv_a.at[i], device_id=device(p), device_id_type=MESH,
            ).start()

        every_owner(send_part)

        def finish_owner():
            mine = pl.ds(pl.multiple_of((me // stride) * rows, rows), rows)
            slots[i, me] = part[i, mine, :]
            settle(slots, count - 1, recv_a)

            def add(p, total):
                return total + slots[i, p]
            full[i, mine, :] = lax.fori_loop(1, count, add, slots[i, 0], unroll=min(count - 1, 31))

            def send_sum(p):
                pltpu.make_async_remote_copy(
                    src_ref=chunk(full, i, me), dst_ref=chunk(full, i, me),
                    send_sem=send_b.at[i], recv_sem=recv_b.at[i], device_id=device(p),
                    device_id_type=MESH,
                ).start()

            everyone(send_sum)
            settle(full, (owners - 1) * rows, send_a)
            settle(full, (owners - 1) * rows, recv_b)
            settle(slots, count - 1, send_b)

        def finish_other():
            settle(full, owners * rows, send_a)
            settle(full, owners * rows, recv_b)

        when_owner(finish_owner, finish_other)

    def step(i, carry):
        sweep(own_count, sc_ref[0:1, 0:1], raw_ref[...], pair_ref, psi_ref, delta_ref, near_ref,
              masked_ref, kinds_ref, raw_ref, part.at[i], slope_ref, pull_ref, rhs_ref, lhs_ref)
        reduce(i)
        advance(lambda z: full[i, z * HALF : (z + 1) * HALF, :], sums, v_ref, w_ref, x_ref,
                pair_ref, sc_ref, raw_ref)
        return carry

    if ROWS > SPECIES * HALF:
        for i in range(ITERS):
            part[i, SPECIES * HALF :, :] = jnp.zeros((ROWS - SPECIES * HALF, LANES), jnp.float32)
    lax.fori_loop(0, ITERS, step, 0)
    for k in range(3):
        left_out[k] = raw_ref[k : k + 1, :own_count]
    at = lax.broadcasted_iota(jnp.int32, (1, 3), 1)
    sc_out[...] = jnp.where(
        at == 0, sc_ref[0:1, 0:1], jnp.where(at == 1, sc_ref[1:2, 0:1], sc_ref[2:3, 0:1]))


def shards(n_snap, n_brick, positions, species, atom_words, left_vector, right_vector, direction,
           solution_in, scalars):
    own_count = positions.shape[2]
    width = own_count + 2 * HALO
    coef_total = float(right_vector.size)
    left_total = float(3 * own_count * n_snap * n_brick * positions.shape[0])
    count = n_snap * n_brick
    owners = min(count, ROWS // 8)
    f32 = jnp.float32

    def shape(*dims):
        return jax.ShapeDtypeStruct(dims, f32)

    def room(*dims):
        return pltpu.VMEM(dims, f32)

    vmem = pl.BlockSpec(memory_space=pltpu.VMEM)
    smem = pl.BlockSpec(memory_space=pltpu.SMEM)
    coefs = shape(SPECIES, CHANNELS, TERMS)
    sem = pltpu.SemaphoreType.DMA
    left_next, v, w, x, sc = pl.pallas_call(
        functools.partial(kernel, n_snap, n_brick, own_count, (left_total, coef_total)),
        out_shape=[shape(3, 1, own_count), coefs, coefs, coefs, shape(1, 3)],
        in_specs=[vmem] * 7 + [smem], out_specs=[vmem] * 5,
        scratch_shapes=[
            room(8, own_count), room(2, 8, LANES), room(8, width), room(2, 16, RADIAL, width),
            room(16, 8, width), room(2, 16, width), room(SPECIES * BLOCK, width), room(8, width),
            room(CHANNELS, width), room(2, 16, RADIAL, width), room(16, width),
            room(CHANNELS, SPECIES * BLOCK), room(8, LANES), room(8, width),
            room(CHANNELS, width), room(2, 16, width), room(CHANNELS, 2 * own_count),
            room(SPECIES * BLOCK, 2 * own_count), room(ITERS, ROWS, LANES),
            room(ITERS, count, ROWS // owners, LANES), room(ITERS, ROWS, LANES),
            sem((2,)), sem((2,)), sem((ITERS,)), sem((ITERS,)), sem((ITERS,)), sem((ITERS,)),
        ],
        compiler_params=pltpu.CompilerParams(
            collective_id=0, has_side_effects=True, vmem_limit_bytes=40 * 2**20),
    )(
        jnp.swapaxes(positions, 0, 1), species, atom_words, jnp.swapaxes(left_vector, 0, 1),
        jnp.swapaxes(right_vector, 1, 2), jnp.swapaxes(direction, 1, 2),
        jnp.swapaxes(solution_in, 1, 2), scalars,
    )
    return (jnp.swapaxes(left_next, 0, 1), jnp.swapaxes(v, 1, 2), jnp.swapaxes(w, 1, 2),
            jnp.swapaxes(x, 1, 2), sc[0])


def solution(mesh):
    placed = (
        P("snap", None, "brick"), P("snap", "brick"), P("snap", "brick"),
        P("snap", None, "brick"), P(), P(), P(), P(),
    )
    return jax.shard_map(
        functools.partial(shards, mesh.shape["snap"], mesh.shape["brick"]),
        mesh=mesh, in_specs=placed,
        out_specs=(P("snap", None, "brick"), P(), P(), P(), P()), check_vma=False,
    )
```

```python
import functools
import math

import jax
import jax.numpy as jnp
from jax import lax
from jax.experimental import pallas as pl
from jax.experimental.pallas import tpu as pltpu
from jax.sharding import PartitionSpec as P

SPECIES = 5
RADIAL = 16
WINDOW = 15
ITERS = 3
CHANNELS = SPECIES * RADIAL
BLOCK = 128
HALF = CHANNELS // 2
TERMS = CHANNELS + 1
MOVE = 128 - TERMS
ROWS = 256
LANES = 128
HALO = 64
INNER = 4

cutoff_sq = 36.0
spacing = 0.25
force_unit = 0.015625
tiny = 1e-06
HIGHEST = lax.Precision.HIGHEST
MESH = pl.DeviceIdType.MESH


def turn(x, shift):
    width = x.shape[1]
    return pltpu.roll(x, shift % width, 1)


def row_sum(x):
    return jnp.sum(x, axis=0, keepdims=True)


def prepare(cells_ref, psi_ref, delta_ref, near_ref, masked_ref, own_ref, dens_ref, phi_ref,
            scaled_ref):
    width = cells_ref.shape[1]
    here = cells_ref[...]
    row_id = lax.broadcasted_iota(jnp.int32, (8, width), 0)
    near_ref[...] = jnp.full(near_ref.shape, -1.0, jnp.float32)
    scaled_ref[...] = jnp.ones(scaled_ref.shape, jnp.float32)
    for o in range(1, WINDOW + 1):
        there = turn(here, -o)
        delta = there - here + jnp.where(row_id == 2, spacing * o, 0.0)
        delta = jnp.where(row_id < 3, delta, 0.0)
        delta_ref[o - 1] = delta
        scaled_ref[o - 1 : o, :] = row_sum(delta * delta)
        near_ref[0, o - 1 : o, :] = there[3:4, :]
        near_ref[1, o - 1 : o, :] = turn(here, o)[3:4, :]
    scaled = scaled_ref[...] / cutoff_sq
    words = jnp.broadcast_to(here[4:5, :].astype(jnp.int32), scaled.shape)
    bits = lax.broadcasted_iota(jnp.int32, scaled.shape, 0)
    linked = jnp.bitwise_and(jnp.right_shift(words, bits), 1).astype(jnp.float32)
    envelope = jnp.maximum(1.0 - scaled, 0.0)
    argument = 2.0 * jnp.minimum(scaled, 1.0) - 1.0
    twice = 2.0 * argument
    square = envelope * envelope * linked
    line = -2.0 * envelope * linked
    first = [jnp.ones_like(argument), argument]
    second = [jnp.ones_like(argument), twice]
    for n in range(RADIAL):
        if n >= 2:
            first.append(twice * first[-1] - first[-2])
            second.append(twice * second[-1] - second[-2])
        damping = 1.0 / (1.0 + n)
        phi = square * first[n] * damping
        psi = line * first[n]
        if n > 0:
            psi = psi + 2.0 * n * square * second[n - 1]
        phi_ref[0, :, n, :] = phi
        psi_ref[0, :, n, :] = psi * damping
    for o in range(1, WINDOW + 1):
        phi_ref[1, o - 1] = turn(phi_ref[0, o - 1], o)
        psi_ref[1, o - 1] = turn(psi_ref[0, o - 1], o)
    kinds = here[3:4, :]
    own_ref[...] = jnp.where(
        jnp.broadcast_to(kinds, (8, width)) == row_id.astype(jnp.float32), 1.0, 0.0
    )
    masked_ref[...] = jnp.zeros(masked_ref.shape, jnp.float32)
    for tile in range(width // LANES):
        at = slice(tile * LANES, (tile + 1) * LANES)
        sums = [jnp.zeros((RADIAL, LANES), jnp.float32) for _ in range(SPECIES)]
        for side in range(2):
            for o in range(WINDOW):
                value = phi_ref[side, o, :, at]
                kind = jnp.broadcast_to(near_ref[side, o : o + 1, at], (RADIAL, LANES))
                for c in range(SPECIES):
                    sums[c] = sums[c] + jnp.where(kind == c, value, 0.0)
        first_row = lax.broadcasted_iota(jnp.int32, (8, LANES), 0) == 0
        for z in range(SPECIES):
            own = own_ref[z : z + 1, at]
            for c in range(SPECIES):
                start = z * BLOCK + c * RADIAL
                masked_ref[start : start + RADIAL, at] = jnp.where(own > 0.5, sums[c], 0.0)
                if z == 0:
                    dens_ref[c * RADIAL : (c + 1) * RADIAL, at] = sums[c]
            start = z * BLOCK + CHANNELS
            masked_ref[start : start + 8, at] = jnp.where(
                first_row, jnp.broadcast_to(own, (8, LANES)), 0.0
            )


def advance(total, sums, v_ref, w_ref, x_ref, pair_ref, sc_ref, raw_ref):
    left_total, coef_total = sums
    back_unit = force_unit * coef_total / left_total
    rho_bar = sc_ref[1:2, 0:1]
    phi_bar = sc_ref[2:3, 0:1]
    beta = jnp.sqrt(total(0)[0:1, TERMS : TERMS + 1] / left_total + tiny)
    scale = back_unit / beta
    lane = lax.broadcasted_iota(jnp.int32, (HALF, LANES), 1)
    wide = lax.broadcasted_iota(jnp.int32, (CHANNELS, LANES), 1)
    last = jnp.where(wide == CHANNELS, 1.0, 0.0)
    once = jnp.where(wide < CHANNELS, 1.0 / math.sqrt(CHANNELS), last) * scale
    twice = jnp.where(wide < CHANNELS, 2.0 / CHANNELS, last) * scale
    power = jnp.zeros((1, TERMS), jnp.float32)
    for z in range(SPECIES):
        at = slice(z * BLOCK, (z + 1) * BLOCK)
        packed = total(z)
        square = jnp.concatenate(
            [packed, jnp.zeros((LANES - HALF, LANES), jnp.float32)], axis=0
        )
        lower = jnp.where(lane < HALF, square.T[HALF:CHANNELS, :], turn(packed, -MOVE))
        back = jnp.concatenate([packed, lower], axis=0)
        v = (once * back)[:, :TERMS] - beta * v_ref[z]
        v_ref[z] = v
        power = power + row_sum(v * v)
        pair_ref[:, at] = twice * back - beta * pair_ref[:, at]
    alpha = jnp.sqrt(jnp.sum(power, axis=1, keepdims=True) / coef_total + tiny)
    rho = jnp.sqrt(rho_bar * rho_bar + beta * beta)
    cosine = rho_bar / rho
    sine = beta / rho
    theta = sine * alpha
    phi = cosine * phi_bar
    inverse = 1.0 / alpha
    for z in range(SPECIES):
        at = slice(z * BLOCK, (z + 1) * BLOCK)
        v = v_ref[z] * inverse
        v_ref[z] = v
        w = w_ref[z]
        x_ref[z] = x_ref[z] + (phi / rho) * w
        w_ref[z] = v - (theta / rho) * w
        pair_ref[:, at] = pair_ref[:, at] * inverse
    raw_ref[...] = raw_ref[...] / beta
    write_scalars(sc_ref, alpha, -cosine * alpha, sine * phi_bar)


def write_scalars(ref, alpha, rho_bar, phi_bar):
    row_id = lax.broadcasted_iota(jnp.int32, ref.shape, 0)
    ref[...] = jnp.where(row_id == 0, alpha, jnp.where(row_id == 1, rho_bar, phi_bar))


def sweep(own_count, alpha, left, pair_ref, psi_ref, delta_ref, near_ref, masked_ref, own_ref,
          raw_ref, out_ref, slope_ref, pull_ref, rhs_ref, lhs_ref):
    width = masked_ref.shape[1]
    unit = 2.0 / cutoff_sq
    slope_ref[...] = jnp.dot(
        pair_ref[...], masked_ref[...], precision=HIGHEST, preferred_element_type=jnp.float32
    )
    for tile in range(width // LANES):
        at = slice(tile * LANES, (tile + 1) * LANES)
        parts = [slope_ref[c * RADIAL : (c + 1) * RADIAL, at] for c in range(SPECIES)]
        for side in range(2):
            for o in range(WINDOW):
                kind = jnp.broadcast_to(near_ref[side, o : o + 1, at], (RADIAL, LANES))
                chosen = parts[0]
                for c in range(1, SPECIES):
                    chosen = jnp.where(kind == c, parts[c], chosen)
                pull_ref[side, o : o + 1, at] = row_sum(chosen * psi_ref[side, o, :, at])
    force = jnp.zeros((8, width), jnp.float32)
    for o in range(1, WINDOW + 1):
        pull = pull_ref[0, o - 1 : o, :] + turn(pull_ref[1, o - 1 : o, :], -o)
        term = (unit * pull) * delta_ref[o - 1]
        force = force + term - turn(term, o)
    raw = force_unit * force - alpha * left
    raw_ref[...] = raw
    for o in range(1, WINDOW + 1):
        project = unit * row_sum(delta_ref[o - 1] * (raw - turn(raw, -o)))
        pull_ref[0, o - 1 : o, :] = project
        pull_ref[1, o - 1 : o, :] = turn(project, o)
    for tile in range(own_count // LANES):
        at = slice(tile * LANES, (tile + 1) * LANES)
        behind = slice(own_count + tile * LANES, own_count + (tile + 1) * LANES)
        sums = [jnp.zeros((RADIAL, LANES), jnp.float32) for _ in range(SPECIES)]
        for side in range(2):
            for o in range(WINDOW):
                value = psi_ref[side, o, :, at] * pull_ref[side, o : o + 1, at]
                kind = jnp.broadcast_to(near_ref[side, o : o + 1, at], (RADIAL, LANES))
                for c in range(SPECIES):
                    sums[c] = sums[c] + jnp.where(kind == c, value, 0.0)
        for c in range(SPECIES):
            rhs_ref[c * RADIAL : (c + 1) * RADIAL, at] = sums[c]
        for z in range(SPECIES):
            own = own_ref[z : z + 1, at]
            for c in range(SPECIES):
                start = z * BLOCK + c * RADIAL
                lhs_ref[start : start + RADIAL, behind] = jnp.where(own > 0.5, sums[c], 0.0)
    cross = lax.dot_general(
        rhs_ref[...], lhs_ref[...], (((1,), (1,)), ((), ())),
        precision=HIGHEST, preferred_element_type=jnp.float32,
    )
    lane = lax.broadcasted_iota(jnp.int32, (HALF, LANES), 1)
    mine = raw[:, :own_count]
    square = jnp.sum(row_sum(mine * mine), axis=1, keepdims=True)
    for z in range(SPECIES):
        block = cross[:, z * BLOCK : (z + 1) * BLOCK]
        upper = jnp.where(lane == TERMS, square, block[:HALF])
        out_ref[z * HALF : (z + 1) * HALF, :] = jnp.where(
            lane < HALF + MOVE, upper, turn(block[HALF:], MOVE))


def kernel(n_snap, n_brick, own_count, sums,
           pos_in, species_in, words_in, left_in, v_in, w_in, x_in, sc_in,
           left_out, v_ref, w_ref, x_ref, sc_out,
           own_ref, ends, cells_ref, psi_ref, delta_ref, near_ref, masked_ref, kinds_ref, dens_ref,
           phi_ref, scaled_ref, pair_ref, sc_ref, raw_ref, slope_ref, pull_ref, rhs_ref, lhs_ref,
           part, slots, lines, full, halo_send, halo_recv, send_a, recv_a, send_b, recv_b, send_c,
           recv_c, load):
    inner = math.gcd(n_brick, INNER)
    plane = n_snap * inner
    depth = n_brick // inner
    rows = ROWS // plane
    snap = lax.axis_index("snap")
    brick = lax.axis_index("brick")
    level = brick // inner
    spot = snap * inner + lax.rem(brick, inner)
    barrier = pltpu.get_barrier_semaphore()

    loads = [pltpu.make_async_copy(source, target, load.at[k]) for k, (source, target) in
             enumerate(((v_in, v_ref), (w_in, w_ref), (x_in, x_ref)))]
    for copy in loads:
        copy.start()

    def in_plane(q):
        return (q // inner, level * inner + lax.rem(q, inner))

    def in_line(q):
        return (snap, q * inner + lax.rem(brick, inner))

    def others(me, count, act):
        if count <= 8:
            for k in range(1, count):
                act(lax.rem(me + k, count))
        else:
            def body(k, carry):
                act(lax.rem(me + k, count))
                return carry
            lax.fori_loop(1, count, body, 0)

    def greet(where):
        pl.semaphore_signal(barrier, inc=1, device_id=where, device_id_type=MESH)

    has_left = brick > 0
    has_right = brick < n_brick - 1
    cross_left = jnp.logical_and(has_left, lax.rem(brick, inner) == 0)
    cross_right = jnp.logical_and(has_right, lax.rem(brick, inner) == inner - 1)
    pl.when(cross_left)(lambda: greet((snap, brick - 1)))
    pl.when(cross_right)(lambda: greet((snap, brick + 1)))
    others(spot, plane, lambda q: greet(in_plane(q)))
    others(level, depth, lambda q: greet(in_line(q)))

    for k in range(3):
        own_ref[k : k + 1, :] = pos_in[k]
        own_ref[5 + k : 6 + k, :] = left_in[k]
    own_ref[3:4, :] = species_in[...].astype(jnp.float32)
    own_ref[4:5, :] = words_in[...].astype(jnp.float32)
    pl.semaphore_wait(
        barrier, plane + depth - 2 + jnp.where(cross_left, 1, 0) + jnp.where(cross_right, 1, 0))

    def shift(step, source, slot):
        return pltpu.make_async_remote_copy(
            src_ref=own_ref.at[:, pl.ds(source, LANES)], dst_ref=ends.at[slot],
            send_sem=halo_send.at[slot], recv_sem=halo_recv.at[slot],
            device_id=(snap, lax.rem(brick + step + n_brick, n_brick)), device_id_type=MESH,
        )

    to_left = shift(-1, 0, 0)
    to_right = shift(1, own_count - LANES, 1)
    pl.when(has_left)(to_left.start)
    pl.when(has_right)(to_right.start)

    write_scalars(sc_ref, sc_in[0], sc_in[1], sc_in[2])
    rhs_ref[...] = jnp.zeros(rhs_ref.shape, jnp.float32)
    lhs_ref[...] = jnp.zeros(lhs_ref.shape, jnp.float32)
    fill = jnp.zeros((CHANNELS, LANES - TERMS), jnp.float32)
    wide = lax.broadcasted_iota(jnp.int32, (CHANNELS, LANES), 1)
    loads[0].wait()
    for z in range(SPECIES):
        v = v_ref[z]
        padded = jnp.concatenate([v, fill], axis=1)
        tall = jnp.concatenate([padded, jnp.zeros((LANES - CHANNELS, LANES), jnp.float32)], axis=0)
        pair = (padded + tall.T[:CHANNELS, :]) * (1.0 / math.sqrt(CHANNELS))
        pair_ref[:, z * BLOCK : (z + 1) * BLOCK] = jnp.where(wide < CHANNELS, pair, padded)

    @pl.when(has_left)
    def _():
        to_left.wait_send()
        to_right.wait_recv()

    @pl.when(has_right)
    def _():
        to_right.wait_send()
        to_left.wait_recv()

    zero = jnp.zeros((8, LANES), jnp.float32)

    @pl.when(jnp.logical_not(has_left))
    def _():
        ends[1] = zero

    @pl.when(jnp.logical_not(has_right))
    def _():
        ends[0] = zero

    cells_ref[:, :own_count] = own_ref[...]
    lane = lax.broadcasted_iota(jnp.int32, (8, LANES), 1)
    cells_ref[:, own_count:] = jnp.where(lane < HALO, ends[0], ends[1])
    prepare(cells_ref, psi_ref, delta_ref, near_ref, masked_ref, kinds_ref, dens_ref, phi_ref,
            scaled_ref)
    raw_ref[...] = jnp.zeros(raw_ref.shape, jnp.float32)
    raw_ref[0:3, :] = cells_ref[5:8, :]
    lhs_ref[:, :own_count] = masked_ref[:, :own_count]
    rhs_ref[:, own_count:] = dens_ref[:, :own_count]

    def chunk(q):
        return pl.ds(pl.multiple_of(q * rows, rows), rows)

    def settle(ref, i, amount, sem):
        view = ref.at[i, pl.ds(0, amount)]
        pltpu.make_async_copy(view, view, sem.at[i]).wait()

    def send(source, target, sent, got, i, where):
        pltpu.make_async_remote_copy(
            src_ref=source, dst_ref=target, send_sem=sent.at[i], recv_sem=got.at[i],
            device_id=where, device_id_type=MESH,
        ).start()

    def add_up(ref, i, count):
        total = ref[i, 0]
        for q in range(1, count):
            total = total + ref[i, q]
        return total

    def reduce(i):
        others(spot, plane, lambda q: send(
            part.at[i, chunk(q)], slots.at[i, spot], send_a, recv_a, i, in_plane(q)))
        slots[i, spot] = part[i, chunk(spot), :]
        settle(slots, i, plane - 1, recv_a)
        lines[i, level] = add_up(slots, i, plane)
        others(level, depth, lambda q: send(
            lines.at[i, level], lines.at[i, level], send_b, recv_b, i, in_line(q)))
        settle(lines, i, depth - 1, recv_b)
        full[i, chunk(spot), :] = add_up(lines, i, depth)
        others(spot, plane, lambda q: send(
            full.at[i, chunk(spot)], full.at[i, chunk(spot)], send_c, recv_c, i, in_plane(q)))
        settle(slots, i, plane - 1, send_a)
        settle(lines, i, depth - 1, send_b)
        settle(slots, i, plane - 1, recv_c)
        settle(slots, i, plane - 1, send_c)

    def step(i, carry):
        sweep(own_count, sc_ref[0:1, 0:1], raw_ref[...], pair_ref, psi_ref, delta_ref, near_ref,
              masked_ref, kinds_ref, raw_ref, part.at[i], slope_ref, pull_ref, rhs_ref, lhs_ref)
        reduce(i)
        advance(lambda z: full[i, z * HALF : (z + 1) * HALF, :], sums, v_ref, w_ref, x_ref,
                pair_ref, sc_ref, raw_ref)
        return carry

    if ROWS > SPECIES * HALF:
        for i in range(ITERS):
            part[i, SPECIES * HALF :, :] = jnp.zeros((ROWS - SPECIES * HALF, LANES), jnp.float32)
    loads[1].wait()
    loads[2].wait()
    lax.fori_loop(0, ITERS, step, 0)
    for k in range(3):
        left_out[k] = raw_ref[k : k + 1, :own_count]
    at = lax.broadcasted_iota(jnp.int32, (1, 3), 1)
    sc_out[...] = jnp.where(
        at == 0, sc_ref[0:1, 0:1], jnp.where(at == 1, sc_ref[1:2, 0:1], sc_ref[2:3, 0:1]))


def store_kernel(*refs):
    copies = [pltpu.make_async_copy(refs[k], refs[5 + k], refs[10].at[k]) for k in range(5)]
    for copy in copies:
        copy.start()
    for copy in copies:
        copy.wait()


def shards(n_snap, n_brick, positions, species, atom_words, left_vector, right_vector, direction,
           solution_in, scalars):
    own_count = positions.shape[2]
    width = own_count + 2 * HALO
    coef_total = float(right_vector.size)
    left_total = float(3 * own_count * n_snap * n_brick * positions.shape[0])
    inner = math.gcd(n_brick, INNER)
    plane = n_snap * inner
    f32 = jnp.float32

    def shape(*dims):
        return jax.ShapeDtypeStruct(dims, f32)

    def room(*dims):
        return pltpu.VMEM(dims, f32)

    vmem = pl.BlockSpec(memory_space=pltpu.VMEM)
    smem = pl.BlockSpec(memory_space=pltpu.SMEM)
    hbm = pl.BlockSpec(memory_space=pltpu.HBM)
    coefs = shape(SPECIES, CHANNELS, TERMS)
    sem = pltpu.SemaphoreType.DMA
    shapes = [shape(3, 1, own_count), coefs, coefs, coefs, shape(1, 3)]
    results = pl.pallas_call(
        functools.partial(kernel, n_snap, n_brick, own_count, (left_total, coef_total)),
        out_shape=shapes,
        in_specs=[vmem] * 4 + [hbm] * 3 + [smem], out_specs=[vmem] * 5,
        scratch_shapes=[
            room(8, own_count), room(2, 8, LANES), room(8, width), room(2, 16, RADIAL, width),
            room(16, 8, width), room(2, 16, width), room(SPECIES * BLOCK, width), room(8, width),
            room(CHANNELS, width), room(2, 16, RADIAL, width), room(16, width),
            room(CHANNELS, SPECIES * BLOCK), room(8, LANES), room(8, width),
            room(CHANNELS, width), room(2, 16, width), room(CHANNELS, 2 * own_count),
            room(SPECIES * BLOCK, 2 * own_count), room(ITERS, ROWS, LANES),
            room(ITERS, plane, ROWS // plane, LANES),
            room(ITERS, n_brick // inner, ROWS // plane, LANES), room(ITERS, ROWS, LANES),
            sem((2,)), sem((2,)), *[sem((ITERS,)) for _ in range(6)], sem((3,)),
        ],
        compiler_params=pltpu.CompilerParams(
            collective_id=0, has_side_effects=True, vmem_limit_bytes=62 * 2**20),
    )(
        jnp.swapaxes(positions, 0, 1), species, atom_words, jnp.swapaxes(left_vector, 0, 1),
        jnp.swapaxes(right_vector, 1, 2), jnp.swapaxes(direction, 1, 2),
        jnp.swapaxes(solution_in, 1, 2), scalars,
    )
    left_next, v, w, x, sc = pl.pallas_call(
        store_kernel, out_shape=shapes, in_specs=[hbm] * 5, out_specs=[hbm] * 5,
        scratch_shapes=[sem((5,))],
        compiler_params=pltpu.CompilerParams(vmem_limit_bytes=62 * 2**20),
    )(*results)
    return (jnp.swapaxes(left_next, 0, 1), jnp.swapaxes(v, 1, 2), jnp.swapaxes(w, 1, 2),
            jnp.swapaxes(x, 1, 2), sc[0])


def solution(mesh):
    placed = (
        P("snap", None, "brick"), P("snap", "brick"), P("snap", "brick"),
        P("snap", None, "brick"), P(), P(), P(), P(),
    )
    return jax.shard_map(
        functools.partial(shards, mesh.shape["snap"], mesh.shape["brick"]),
        mesh=mesh, in_specs=placed,
        out_specs=(P("snap", None, "brick"), P(), P(), P(), P()), check_vma=False,
    )
```

```python
import functools
import math

import jax
import jax.numpy as jnp
from jax import lax
from jax.experimental import pallas as pl
from jax.experimental.pallas import tpu as pltpu
from jax.sharding import PartitionSpec as P

SPECIES = 5
RADIAL = 16
WINDOW = 15
ITERS = 3
CHANNELS = SPECIES * RADIAL
BLOCK = 128
HALF = CHANNELS // 2
TERMS = CHANNELS + 1
MOVE = 128 - TERMS
ROWS = 256
LANES = 128
HALO = 64
INNER = 4

cutoff_sq = 36.0
spacing = 0.25
force_unit = 0.015625
tiny = 1e-06
MESH = pl.DeviceIdType.MESH


def turn(x, shift):
    width = x.shape[1]
    return pltpu.roll(x, shift % width, 1)


def row_sum(x):
    return jnp.sum(x, axis=0, keepdims=True)


def product(x, y, dims):
    def halves(a):
        high = a.astype(jnp.bfloat16)
        return high, (a - high.astype(jnp.float32)).astype(jnp.bfloat16)

    def dot(a, b):
        return lax.dot_general(a, b, (dims, ((), ())), preferred_element_type=jnp.float32)

    x_high, x_low = halves(x)
    y_high, y_low = halves(y)
    return dot(x_high, y_high) + (dot(x_high, y_low) + dot(x_low, y_high))


def prepare(cells_ref, psi_ref, delta_ref, near_ref, masked_ref, own_ref, dens_ref, phi_ref,
            scaled_ref):
    width = cells_ref.shape[1]
    here = cells_ref[...]
    row_id = lax.broadcasted_iota(jnp.int32, (8, width), 0)
    near_ref[...] = jnp.full(near_ref.shape, -1.0, jnp.float32)
    scaled_ref[...] = jnp.ones(scaled_ref.shape, jnp.float32)
    for o in range(1, WINDOW + 1):
        there = turn(here, -o)
        delta = there - here + jnp.where(row_id == 2, spacing * o, 0.0)
        delta = jnp.where(row_id < 3, delta, 0.0)
        delta_ref[o - 1] = delta
        scaled_ref[o - 1 : o, :] = row_sum(delta * delta)
        near_ref[0, o - 1 : o, :] = there[3:4, :]
        near_ref[1, o - 1 : o, :] = turn(here, o)[3:4, :]
    scaled = scaled_ref[...] / cutoff_sq
    words = jnp.broadcast_to(here[4:5, :].astype(jnp.int32), scaled.shape)
    bits = lax.broadcasted_iota(jnp.int32, scaled.shape, 0)
    linked = jnp.bitwise_and(jnp.right_shift(words, bits), 1).astype(jnp.float32)
    envelope = jnp.maximum(1.0 - scaled, 0.0)
    argument = 2.0 * jnp.minimum(scaled, 1.0) - 1.0
    twice = 2.0 * argument
    square = envelope * envelope * linked
    line = -2.0 * envelope * linked
    first = [jnp.ones_like(argument), argument]
    second = [jnp.ones_like(argument), twice]
    for n in range(RADIAL):
        if n >= 2:
            first.append(twice * first[-1] - first[-2])
            second.append(twice * second[-1] - second[-2])
        damping = 1.0 / (1.0 + n)
        phi = square * first[n] * damping
        psi = line * first[n]
        if n > 0:
            psi = psi + 2.0 * n * square * second[n - 1]
        phi_ref[0, :, n, :] = phi
        psi_ref[0, :, n, :] = psi * damping
    for o in range(1, WINDOW + 1):
        phi_ref[1, o - 1] = turn(phi_ref[0, o - 1], o)
        psi_ref[1, o - 1] = turn(psi_ref[0, o - 1], o)
    kinds = here[3:4, :]
    own_ref[...] = jnp.where(
        jnp.broadcast_to(kinds, (8, width)) == row_id.astype(jnp.float32), 1.0, 0.0
    )
    masked_ref[...] = jnp.zeros(masked_ref.shape, jnp.float32)
    for tile in range(width // LANES):
        at = slice(tile * LANES, (tile + 1) * LANES)
        sums = [jnp.zeros((RADIAL, LANES), jnp.float32) for _ in range(SPECIES)]
        for side in range(2):
            for o in range(WINDOW):
                value = phi_ref[side, o, :, at]
                kind = jnp.broadcast_to(near_ref[side, o : o + 1, at], (RADIAL, LANES))
                for c in range(SPECIES):
                    sums[c] = sums[c] + jnp.where(kind == c, value, 0.0)
        first_row = lax.broadcasted_iota(jnp.int32, (8, LANES), 0) == 0
        for z in range(SPECIES):
            own = own_ref[z : z + 1, at]
            for c in range(SPECIES):
                start = z * BLOCK + c * RADIAL
                masked_ref[start : start + RADIAL, at] = jnp.where(own > 0.5, sums[c], 0.0)
                if z == 0:
                    dens_ref[c * RADIAL : (c + 1) * RADIAL, at] = sums[c]
            start = z * BLOCK + CHANNELS
            masked_ref[start : start + 8, at] = jnp.where(
                first_row, jnp.broadcast_to(own, (8, LANES)), 0.0
            )


def advance(total, sums, v_ref, w_ref, x_ref, pair_ref, sc_ref, raw_ref):
    left_total, coef_total = sums
    back_unit = force_unit * coef_total / left_total
    rho_bar = sc_ref[1:2, 0:1]
    phi_bar = sc_ref[2:3, 0:1]
    beta = jnp.sqrt(total(0)[0:1, TERMS : TERMS + 1] / left_total + tiny)
    scale = back_unit / beta
    lane = lax.broadcasted_iota(jnp.int32, (HALF, LANES), 1)
    wide = lax.broadcasted_iota(jnp.int32, (CHANNELS, LANES), 1)
    last = jnp.where(wide == CHANNELS, 1.0, 0.0)
    once = jnp.where(wide < CHANNELS, 1.0 / math.sqrt(CHANNELS), last) * scale
    twice = jnp.where(wide < CHANNELS, 2.0 / CHANNELS, last) * scale
    power = jnp.zeros((1, TERMS), jnp.float32)
    for z in range(SPECIES):
        at = slice(z * BLOCK, (z + 1) * BLOCK)
        packed = total(z)
        square = jnp.concatenate(
            [packed, jnp.zeros((LANES - HALF, LANES), jnp.float32)], axis=0
        )
        lower = jnp.where(lane < HALF, square.T[HALF:CHANNELS, :], turn(packed, -MOVE))
        back = jnp.concatenate([packed, lower], axis=0)
        v = (once * back)[:, :TERMS] - beta * v_ref[z]
        v_ref[z] = v
        power = power + row_sum(v * v)
        pair_ref[:, at] = twice * back - beta * pair_ref[:, at]
    alpha = jnp.sqrt(jnp.sum(power, axis=1, keepdims=True) / coef_total + tiny)
    rho = jnp.sqrt(rho_bar * rho_bar + beta * beta)
    cosine = rho_bar / rho
    sine = beta / rho
    theta = sine * alpha
    phi = cosine * phi_bar
    inverse = 1.0 / alpha
    for z in range(SPECIES):
        at = slice(z * BLOCK, (z + 1) * BLOCK)
        v = v_ref[z] * inverse
        v_ref[z] = v
        w = w_ref[z]
        x_ref[z] = x_ref[z] + (phi / rho) * w
        w_ref[z] = v - (theta / rho) * w
        pair_ref[:, at] = pair_ref[:, at] * inverse
    raw_ref[...] = raw_ref[...] / beta
    write_scalars(sc_ref, alpha, -cosine * alpha, sine * phi_bar)


def write_scalars(ref, alpha, rho_bar, phi_bar):
    row_id = lax.broadcasted_iota(jnp.int32, ref.shape, 0)
    ref[...] = jnp.where(row_id == 0, alpha, jnp.where(row_id == 1, rho_bar, phi_bar))


def sweep(own_count, alpha, left, pair_ref, psi_ref, delta_ref, near_ref, masked_ref, own_ref,
          raw_ref, out_ref, slope_ref, pull_ref, rhs_ref, lhs_ref):
    width = masked_ref.shape[1]
    unit = 2.0 / cutoff_sq
    slope_ref[...] = product(pair_ref[...], masked_ref[...], ((1,), (0,)))
    for tile in range(width // LANES):
        at = slice(tile * LANES, (tile + 1) * LANES)
        parts = [slope_ref[c * RADIAL : (c + 1) * RADIAL, at] for c in range(SPECIES)]
        for side in range(2):
            for o in range(WINDOW):
                kind = jnp.broadcast_to(near_ref[side, o : o + 1, at], (RADIAL, LANES))
                chosen = parts[0]
                for c in range(1, SPECIES):
                    chosen = jnp.where(kind == c, parts[c], chosen)
                pull_ref[side, o : o + 1, at] = row_sum(chosen * psi_ref[side, o, :, at])
    force = jnp.zeros((8, width), jnp.float32)
    for o in range(1, WINDOW + 1):
        pull = pull_ref[0, o - 1 : o, :] + turn(pull_ref[1, o - 1 : o, :], -o)
        term = (unit * pull) * delta_ref[o - 1]
        force = force + term - turn(term, o)
    raw = force_unit * force - alpha * left
    raw_ref[...] = raw
    for o in range(1, WINDOW + 1):
        project = unit * row_sum(delta_ref[o - 1] * (raw - turn(raw, -o)))
        pull_ref[0, o - 1 : o, :] = project
        pull_ref[1, o - 1 : o, :] = turn(project, o)
    for tile in range(own_count // LANES):
        at = slice(tile * LANES, (tile + 1) * LANES)
        behind = slice(own_count + tile * LANES, own_count + (tile + 1) * LANES)
        sums = [jnp.zeros((RADIAL, LANES), jnp.float32) for _ in range(SPECIES)]
        for side in range(2):
            for o in range(WINDOW):
                value = psi_ref[side, o, :, at] * pull_ref[side, o : o + 1, at]
                kind = jnp.broadcast_to(near_ref[side, o : o + 1, at], (RADIAL, LANES))
                for c in range(SPECIES):
                    sums[c] = sums[c] + jnp.where(kind == c, value, 0.0)
        for c in range(SPECIES):
            rhs_ref[c * RADIAL : (c + 1) * RADIAL, at] = sums[c]
        for z in range(SPECIES):
            own = own_ref[z : z + 1, at]
            for c in range(SPECIES):
                start = z * BLOCK + c * RADIAL
                lhs_ref[start : start + RADIAL, behind] = jnp.where(own > 0.5, sums[c], 0.0)
    cross = product(rhs_ref[...], lhs_ref[...], ((1,), (1,)))
    lane = lax.broadcasted_iota(jnp.int32, (HALF, LANES), 1)
    mine = raw[:, :own_count]
    square = jnp.sum(row_sum(mine * mine), axis=1, keepdims=True)
    for z in range(SPECIES):
        block = cross[:, z * BLOCK : (z + 1) * BLOCK]
        upper = jnp.where(lane == TERMS, square, block[:HALF])
        out_ref[z * HALF : (z + 1) * HALF, :] = jnp.where(
            lane < HALF + MOVE, upper, turn(block[HALF:], MOVE))


def kernel(n_snap, n_brick, own_count, sums,
           pos_in, species_in, words_in, left_in, v_in, w_in, x_in, sc_in,
           left_out, v_ref, w_ref, x_ref, sc_out,
           own_ref, ends, cells_ref, psi_ref, delta_ref, near_ref, masked_ref, kinds_ref, dens_ref,
           phi_ref, scaled_ref, pair_ref, sc_ref, raw_ref, slope_ref, pull_ref, rhs_ref, lhs_ref,
           part, slots, lines, full, halo_send, halo_recv, send_a, recv_a, send_b, recv_b, send_c,
           recv_c, load):
    inner = math.gcd(n_brick, INNER)
    plane = n_snap * inner
    depth = n_brick // inner
    rows = ROWS // plane
    snap = lax.axis_index("snap")
    brick = lax.axis_index("brick")
    level = brick // inner
    spot = snap * inner + lax.rem(brick, inner)
    barrier = pltpu.get_barrier_semaphore()

    loads = [pltpu.make_async_copy(source, target, load.at[k]) for k, (source, target) in
             enumerate(((v_in, v_ref), (w_in, w_ref), (x_in, x_ref)))]
    for copy in loads:
        copy.start()

    def in_plane(q):
        return (q // inner, level * inner + lax.rem(q, inner))

    def in_line(q):
        return (snap, q * inner + lax.rem(brick, inner))

    def others(me, count, act):
        if count <= 8:
            for k in range(1, count):
                act(lax.rem(me + k, count))
        else:
            def body(k, carry):
                act(lax.rem(me + k, count))
                return carry
            lax.fori_loop(1, count, body, 0)

    def greet(where):
        pl.semaphore_signal(barrier, inc=1, device_id=where, device_id_type=MESH)

    has_left = brick > 0
    has_right = brick < n_brick - 1
    cross_left = jnp.logical_and(has_left, lax.rem(brick, inner) == 0)
    cross_right = jnp.logical_and(has_right, lax.rem(brick, inner) == inner - 1)
    pl.when(cross_left)(lambda: greet((snap, brick - 1)))
    pl.when(cross_right)(lambda: greet((snap, brick + 1)))
    others(spot, plane, lambda q: greet(in_plane(q)))
    others(level, depth, lambda q: greet(in_line(q)))

    for k in range(3):
        own_ref[k : k + 1, :] = pos_in[k]
        own_ref[5 + k : 6 + k, :] = left_in[k]
    own_ref[3:4, :] = species_in[...].astype(jnp.float32)
    own_ref[4:5, :] = words_in[...].astype(jnp.float32)
    pl.semaphore_wait(
        barrier, plane + depth - 2 + jnp.where(cross_left, 1, 0) + jnp.where(cross_right, 1, 0))

    def shift(step, source, slot):
        return pltpu.make_async_remote_copy(
            src_ref=own_ref.at[:, pl.ds(source, LANES)], dst_ref=ends.at[slot],
            send_sem=halo_send.at[slot], recv_sem=halo_recv.at[slot],
            device_id=(snap, lax.rem(brick + step + n_brick, n_brick)), device_id_type=MESH,
        )

    to_left = shift(-1, 0, 0)
    to_right = shift(1, own_count - LANES, 1)
    pl.when(has_left)(to_left.start)
    pl.when(has_right)(to_right.start)

    write_scalars(sc_ref, sc_in[0], sc_in[1], sc_in[2])
    rhs_ref[...] = jnp.zeros(rhs_ref.shape, jnp.float32)
    lhs_ref[...] = jnp.zeros(lhs_ref.shape, jnp.float32)
    fill = jnp.zeros((CHANNELS, LANES - TERMS), jnp.float32)
    wide = lax.broadcasted_iota(jnp.int32, (CHANNELS, LANES), 1)
    loads[0].wait()
    for z in range(SPECIES):
        v = v_ref[z]
        padded = jnp.concatenate([v, fill], axis=1)
        tall = jnp.concatenate([padded, jnp.zeros((LANES - CHANNELS, LANES), jnp.float32)], axis=0)
        pair = (padded + tall.T[:CHANNELS, :]) * (1.0 / math.sqrt(CHANNELS))
        pair_ref[:, z * BLOCK : (z + 1) * BLOCK] = jnp.where(wide < CHANNELS, pair, padded)

    @pl.when(has_left)
    def _():
        to_left.wait_send()
        to_right.wait_recv()

    @pl.when(has_right)
    def _():
        to_right.wait_send()
        to_left.wait_recv()

    zero = jnp.zeros((8, LANES), jnp.float32)

    @pl.when(jnp.logical_not(has_left))
    def _():
        ends[1] = zero

    @pl.when(jnp.logical_not(has_right))
    def _():
        ends[0] = zero

    cells_ref[:, :own_count] = own_ref[...]
    lane = lax.broadcasted_iota(jnp.int32, (8, LANES), 1)
    cells_ref[:, own_count:] = jnp.where(lane < HALO, ends[0], ends[1])
    prepare(cells_ref, psi_ref, delta_ref, near_ref, masked_ref, kinds_ref, dens_ref, phi_ref,
            scaled_ref)
    raw_ref[...] = jnp.zeros(raw_ref.shape, jnp.float32)
    raw_ref[0:3, :] = cells_ref[5:8, :]
    lhs_ref[:, :own_count] = masked_ref[:, :own_count]
    rhs_ref[:, own_count:] = dens_ref[:, :own_count]

    def chunk(q):
        return pl.ds(pl.multiple_of(q * rows, rows), rows)

    def settle(ref, i, amount, sem):
        view = ref.at[i, pl.ds(0, amount)]
        pltpu.make_async_copy(view, view, sem.at[i]).wait()

    def send(source, target, sent, got, i, where):
        pltpu.make_async_remote_copy(
            src_ref=source, dst_ref=target, send_sem=sent.at[i], recv_sem=got.at[i],
            device_id=where, device_id_type=MESH,
        ).start()

    def add_up(ref, i, count):
        total = ref[i, 0]
        for q in range(1, count):
            total = total + ref[i, q]
        return total

    def reduce(i):
        others(spot, plane, lambda q: send(
            part.at[i, chunk(q)], slots.at[i, spot], send_a, recv_a, i, in_plane(q)))
        slots[i, spot] = part[i, chunk(spot), :]
        settle(slots, i, plane - 1, recv_a)
        lines[i, level] = add_up(slots, i, plane)
        others(level, depth, lambda q: send(
            lines.at[i, level], lines.at[i, level], send_b, recv_b, i, in_line(q)))
        settle(lines, i, depth - 1, recv_b)
        full[i, chunk(spot), :] = add_up(lines, i, depth)
        others(spot, plane, lambda q: send(
            full.at[i, chunk(spot)], full.at[i, chunk(spot)], send_c, recv_c, i, in_plane(q)))
        settle(slots, i, plane - 1, send_a)
        settle(lines, i, depth - 1, send_b)
        settle(slots, i, plane - 1, recv_c)
        settle(slots, i, plane - 1, send_c)

    def step(i, carry):
        sweep(own_count, sc_ref[0:1, 0:1], raw_ref[...], pair_ref, psi_ref, delta_ref, near_ref,
              masked_ref, kinds_ref, raw_ref, part.at[i], slope_ref, pull_ref, rhs_ref, lhs_ref)
        reduce(i)
        advance(lambda z: full[i, z * HALF : (z + 1) * HALF, :], sums, v_ref, w_ref, x_ref,
                pair_ref, sc_ref, raw_ref)
        return carry

    if ROWS > SPECIES * HALF:
        for i in range(ITERS):
            part[i, SPECIES * HALF :, :] = jnp.zeros((ROWS - SPECIES * HALF, LANES), jnp.float32)
    loads[1].wait()
    loads[2].wait()
    lax.fori_loop(0, ITERS, step, 0)
    for k in range(3):
        left_out[k] = raw_ref[k : k + 1, :own_count]
    at = lax.broadcasted_iota(jnp.int32, (1, 3), 1)
    sc_out[...] = jnp.where(
        at == 0, sc_ref[0:1, 0:1], jnp.where(at == 1, sc_ref[1:2, 0:1], sc_ref[2:3, 0:1]))


def store_kernel(*refs):
    loads = [pltpu.make_async_copy(refs[k], refs[10 + k], refs[15].at[k]) for k in range(5)]
    stores = [pltpu.make_async_copy(refs[10 + k], refs[5 + k], refs[16].at[k]) for k in range(5)]
    for copy in loads:
        copy.start()
    for load, store in zip(loads, stores):
        load.wait()
        store.start()
    for copy in stores:
        copy.wait()


def shards(n_snap, n_brick, positions, species, atom_words, left_vector, right_vector, direction,
           solution_in, scalars):
    own_count = positions.shape[2]
    width = own_count + 2 * HALO
    coef_total = float(right_vector.size)
    left_total = float(3 * own_count * n_snap * n_brick * positions.shape[0])
    inner = math.gcd(n_brick, INNER)
    plane = n_snap * inner
    f32 = jnp.float32

    def shape(*dims):
        return jax.ShapeDtypeStruct(dims, f32)

    def room(*dims):
        return pltpu.VMEM(dims, f32)

    vmem = pl.BlockSpec(memory_space=pltpu.VMEM)
    smem = pl.BlockSpec(memory_space=pltpu.SMEM)
    hbm = pl.BlockSpec(memory_space=pltpu.HBM)
    coefs = shape(SPECIES, CHANNELS, TERMS)
    sem = pltpu.SemaphoreType.DMA
    shapes = [shape(3, 1, own_count), coefs, coefs, coefs, shape(1, 3)]
    results = pl.pallas_call(
        functools.partial(kernel, n_snap, n_brick, own_count, (left_total, coef_total)),
        out_shape=shapes,
        in_specs=[vmem] * 4 + [hbm] * 3 + [smem], out_specs=[vmem] * 5,
        scratch_shapes=[
            room(8, own_count), room(2, 8, LANES), room(8, width), room(2, 16, RADIAL, width),
            room(16, 8, width), room(2, 16, width), room(SPECIES * BLOCK, width), room(8, width),
            room(CHANNELS, width), room(2, 16, RADIAL, width), room(16, width),
            room(CHANNELS, SPECIES * BLOCK), room(8, LANES), room(8, width),
            room(CHANNELS, width), room(2, 16, width), room(CHANNELS, 2 * own_count),
            room(SPECIES * BLOCK, 2 * own_count), room(ITERS, ROWS, LANES),
            room(ITERS, plane, ROWS // plane, LANES),
            room(ITERS, n_brick // inner, ROWS // plane, LANES), room(ITERS, ROWS, LANES),
            sem((2,)), sem((2,)), *[sem((ITERS,)) for _ in range(6)], sem((3,)),
        ],
        compiler_params=pltpu.CompilerParams(
            collective_id=0, has_side_effects=True, vmem_limit_bytes=62 * 2**20),
    )(
        jnp.swapaxes(positions, 0, 1), species, atom_words, jnp.swapaxes(left_vector, 0, 1),
        jnp.swapaxes(right_vector, 1, 2), jnp.swapaxes(direction, 1, 2),
        jnp.swapaxes(solution_in, 1, 2), scalars,
    )
    left_next, v, w, x, sc = pl.pallas_call(
        store_kernel, out_shape=shapes, in_specs=[hbm] * 5, out_specs=[hbm] * 5,
        scratch_shapes=[room(*one.shape) for one in shapes] + [sem((5,)), sem((5,))],
        compiler_params=pltpu.CompilerParams(vmem_limit_bytes=62 * 2**20),
    )(*results)
    return (jnp.swapaxes(left_next, 0, 1), jnp.swapaxes(v, 1, 2), jnp.swapaxes(w, 1, 2),
            jnp.swapaxes(x, 1, 2), sc[0])


def solution(mesh):
    placed = (
        P("snap", None, "brick"), P("snap", "brick"), P("snap", "brick"),
        P("snap", None, "brick"), P(), P(), P(), P(),
    )
    return jax.shard_map(
        functools.partial(shards, mesh.shape["snap"], mesh.shape["brick"]),
        mesh=mesh, in_specs=placed,
        out_specs=(P("snap", None, "brick"), P(), P(), P(), P()), check_vma=False,
    )
```
